128 devices in a mesh: dp: 8 (over y_hi, z), ctx: 16 (over x, y_lo, core).
Axes of the slice: x: 4, y: 4 (y_hi: 2, y_lo: 2; y = y_hi * 2 + y_lo), z: 4, core: 2. Of those that a mesh axis runs over, the one named last changes fastest.
Arguments:
- queries: bfloat16 [8, 2048, 4096], P('dp', 'ctx'), may hold values from -6 to 6
- key_tensor: bfloat16 [8, 2048, 512], P('dp', 'ctx'), may hold values from -6 to 6
- value_tensor: bfloat16 [8, 2048, 512], P('dp', 'ctx'), may hold values from -6 to 6
- attention_output: bfloat16 [8, 2048, 4096], P('dp', 'ctx'), may hold values from -6 to 6
- output_gradient: bfloat16 [8, 2048, 4096], P('dp', 'ctx'), may hold values from -0.59765625 to 0.59765625
- logsumexp_rows: float32 [8, 32, 2048], P('dp', None, 'ctx'), may hold values from 1 to 5
- layer_input: bfloat16 [8, 2048, 5120], P('dp', 'ctx'), may hold values from -6 to 6
- parents: int32 [8, 16], P('dp'), may hold values from 0 to 14, as said below
Outputs:
- grad_queries: bfloat16 [8, 2048, 4096], P('dp', 'ctx')
- grad_keys: bfloat16 [8, 2048, 512], P('dp', 'ctx')
- grad_values: bfloat16 [8, 2048, 512], P('dp', 'ctx')
- grad_kv_weight: float32 [5120, 1024], P(('dp', 'ctx'))
The draws below stay inside these ranges and needn't reach their ends.
Inputs may be any that keep to these rules, and one draw needn't show every extreme that they name: parents[0] is 0 (the root); for every block b >= 1 of a tree parents[b] < b; the last block's parent is the block before it.
All inputs are finite; a program needn't handle non-finite values.
Results may differ from the reference program's by a relative error of at most 0.0057.
Values may be sent and summed in bfloat16 or wider, within the bound.
No kernel may reach another device: no remote copies, remote signals or barrier semaphores. Data moves between devices by JAX's collectives and lax.ppermute only.
A program may use at most 128 MiB of HBM per device.

```python
import math
import jax
import jax.numpy as jnp
from jax import lax

D = 5120
QUERY_HEADS = 32
KEY_VALUE_HEADS = 4
HEAD_SIZE = 128
BLK = 128
TREE_TOKENS = 2048
NBLK = 16
TREE_COUNT = 8


def draw_parents(key, part):
    key = jax.random.fold_in(key, 7)
    jump_key, pick_key = jax.random.split(key)
    block_ids = jnp.arange(NBLK, dtype=jnp.int32)
    jumps = jax.random.randint(jump_key, (TREE_COUNT, NBLK), 0, jnp.maximum(block_ids, 1))
    picks = jax.random.randint(pick_key, (TREE_COUNT, NBLK), 0, 4)
    chained = jnp.maximum(block_ids - 1, 0)
    parent_rows = jnp.where(picks == 0, jumps, chained[None, :])
    parent_rows = jnp.where(block_ids[None, :] == NBLK - 1, NBLK - 2, parent_rows)
    return parent_rows.astype(jnp.int32)


def strengthened(drawn, own_key, source, target, blocks, factor):
    owner, partner = [(jnp.arange(drawn.shape[dim]) // (drawn.shape[dim] // blocks)).reshape([-1 if axis == dim else 1 for axis in range(drawn.ndim)]) for dim in (source, target)]
    chosen = jax.random.permutation(own_key, blocks)[partner]
    strong = (owner == chosen) | (owner == (partner + blocks // 2) % blocks)
    return jnp.where(strong, factor * drawn, drawn)


def shard_levels(key, dims, pieces, least, high):
    gain = 1.0
    for axis_at, shards_of in pieces:
        draws = jax.random.uniform(jax.random.fold_in(jax.random.fold_in(key, 6), axis_at), (shards_of,), jnp.float32, least / len(pieces), high / len(pieces))
        gain = gain * jnp.repeat(jnp.exp(draws), dims[axis_at] // shards_of).reshape((-1,) + (1,) * (len(dims) - 1 - axis_at))
    return gain


def centred(stream_key, shape, scale, reach, cuts=(), kind=jnp.bfloat16):
    values = scale * jax.random.normal(stream_key, shape, jnp.float32)
    if cuts:
        values = values * shard_levels(stream_key, shape, cuts, -0.22, 0.18)
    return jnp.clip(values, -reach, reach).astype(kind)


def heavy_noise(own_key, shape, spread, bound, shards, heavy, kind=jnp.bfloat16):
    values = spread * jax.random.normal(own_key, shape, jnp.float32)
    if shards:
        values = values * shard_levels(own_key, shape, shards, -0.22, 0.18)
    return jnp.clip(strengthened(values, jax.random.fold_in(own_key, 3), *heavy), -bound, bound).astype(kind)


def setup_inputs(seed: int = 0) -> dict:
    keys = jax.random.split(jax.random.key(seed), 9)
    return {
        "queries": centred(keys[0], (TREE_COUNT, TREE_TOKENS, QUERY_HEADS * HEAD_SIZE), 1.0, 6.0, ((0, 8), (1, 16))),
        "key_tensor": centred(keys[1], (TREE_COUNT, TREE_TOKENS, KEY_VALUE_HEADS * HEAD_SIZE), 1.0, 6.0, ((0, 8), (1, 16))),
        "value_tensor": centred(keys[2], (TREE_COUNT, TREE_TOKENS, KEY_VALUE_HEADS * HEAD_SIZE), 1.0, 6.0, ((0, 8), (1, 16))),
        "attention_output": centred(keys[3], (TREE_COUNT, TREE_TOKENS, QUERY_HEADS * HEAD_SIZE), 1.0, 6.0, ((0, 8), (1, 16))),
        "output_gradient": centred(keys[4], (TREE_COUNT, TREE_TOKENS, QUERY_HEADS * HEAD_SIZE), 0.1, 0.59765625, ((0, 8), (1, 16))),
        "logsumexp_rows": jnp.clip(1.0 + 4.0 * jax.random.uniform(keys[5], (TREE_COUNT, QUERY_HEADS, TREE_TOKENS), jnp.float32) ** shard_levels(keys[5], (TREE_COUNT, QUERY_HEADS, TREE_TOKENS), ((0, 8), (2, 16)), -0.2, 0.2), 1.0, 5.0),
        "layer_input": heavy_noise(keys[6], (TREE_COUNT, TREE_TOKENS, D), 1.0, 6.0, ((0, 8), (1, 16)), (1, 2, 16, 2.0)),
        "parents": draw_parents(jax.random.fold_in(keys[8], 71), 0),
    }


def ancestry(parent_row, block_count):
    block_ids = jnp.arange(block_count, dtype=jnp.int32)
    parent_hop = ((parent_row[:, None] == block_ids[None, :]) & (block_ids[:, None] > 0)).astype(jnp.float32)
    reach_table = jnp.maximum(jnp.eye(block_count, dtype=jnp.float32), parent_hop)
    for level in range(block_count.bit_length()):
        reach_table = jnp.minimum(jnp.dot(reach_table, reach_table, precision=lax.Precision.HIGHEST), 1.0)
    return reach_table


def reference(queries, key_tensor, value_tensor, attention_output, output_gradient, logsumexp_rows, layer_input, parents):
    block_count = parents.shape[1]
    query_group_width = QUERY_HEADS // KEY_VALUE_HEADS
    score_scale = HEAD_SIZE ** -0.5
    query_tile_block = math.gcd(TREE_TOKENS, 256)
    key_value_width = KEY_VALUE_HEADS * HEAD_SIZE

    def per_tree(grad_acc, tree_data):
        query_row_view, key_row_view, value_row_view, output_row_view, gradient_row_view, logsumexp_row_view, input_rows, parent_row = tree_data
        reach_table = ancestry(parent_row, block_count)
        key_complete = key_row_view.reshape(TREE_TOKENS, KEY_VALUE_HEADS, HEAD_SIZE).astype(jnp.float32)
        value_complete = value_row_view.reshape(TREE_TOKENS, KEY_VALUE_HEADS, HEAD_SIZE).astype(jnp.float32)
        key_pos = jnp.arange(TREE_TOKENS, dtype=jnp.int32)
        key_blk = key_pos // BLK

        def per_block(grad_pair, row_offset):
            key_acc, value_acc = grad_pair
            query_by_head = lax.dynamic_slice_in_dim(query_row_view, row_offset, query_tile_block, 0).reshape(query_tile_block, KEY_VALUE_HEADS, query_group_width, HEAD_SIZE).astype(jnp.float32)
            gradient_by_head = lax.dynamic_slice_in_dim(gradient_row_view, row_offset, query_tile_block, 0).reshape(query_tile_block, KEY_VALUE_HEADS, query_group_width, HEAD_SIZE).astype(jnp.float32)
            output_by_head = lax.dynamic_slice_in_dim(output_row_view, row_offset, query_tile_block, 0).reshape(query_tile_block, KEY_VALUE_HEADS, query_group_width, HEAD_SIZE).astype(jnp.float32)
            logsumexp_block = lax.dynamic_slice_in_dim(logsumexp_row_view, row_offset, query_tile_block, 1).reshape(KEY_VALUE_HEADS, query_group_width, query_tile_block)
            query_pos = row_offset + jnp.arange(query_tile_block, dtype=jnp.int32)
            query_blk = query_pos // BLK
            reach_rows = reach_table[query_blk][:, key_blk]
            allowed = (reach_rows > 0.5) & ((query_blk[:, None] != key_blk[None, :]) | (key_pos[None, :] <= query_pos[:, None]))
            row_delta = jnp.sum(gradient_by_head * output_by_head, axis=-1).transpose(1, 2, 0)
            scores = jnp.einsum("tkgd,nkd->kgtn", query_by_head, key_complete) * score_scale
            prob_full = jnp.where(allowed[None, None], jnp.exp(scores - logsumexp_block[..., None]), 0.0)
            prob_low = lax.optimization_barrier(prob_full.astype(jnp.bfloat16)).astype(jnp.float32)
            prob_grad = jnp.einsum("tkgd,nkd->kgtn", gradient_by_head, value_complete)
            dscore = prob_full * (prob_grad - row_delta[..., None])
            dscore_low = lax.optimization_barrier(dscore.astype(jnp.bfloat16)).astype(jnp.float32)
            query_grad = (jnp.einsum("kgtn,nkd->tkgd", dscore_low, key_complete) * score_scale).astype(jnp.bfloat16)
            key_acc = key_acc + jnp.einsum("kgtn,tkgd->nkd", dscore_low, query_by_head) * score_scale
            value_acc = value_acc + jnp.einsum("kgtn,tkgd->nkd", prob_low, gradient_by_head)
            return (key_acc, value_acc), query_grad.reshape(query_tile_block, QUERY_HEADS * HEAD_SIZE)

        starts = jnp.arange(TREE_TOKENS // query_tile_block, dtype=jnp.int32) * query_tile_block
        initial_gradients = jnp.zeros((TREE_TOKENS, KEY_VALUE_HEADS, HEAD_SIZE), jnp.float32)
        (key_acc, value_acc), query_parts = lax.scan(per_block, (initial_gradients, initial_gradients), starts)
        query_grads = query_parts.reshape(TREE_TOKENS, QUERY_HEADS * HEAD_SIZE)
        key_low = key_acc.reshape(TREE_TOKENS, key_value_width).astype(jnp.bfloat16)
        value_low = value_acc.reshape(TREE_TOKENS, key_value_width).astype(jnp.bfloat16)
        kv_grads = jnp.concatenate([key_low, value_low], axis=1)
        grad_acc = grad_acc + lax.dot_general(input_rows, kv_grads, (((0,), (0,)), ((), ())), preferred_element_type=jnp.float32)
        return grad_acc, (query_grads, key_low, value_low)

    weight_zero = jnp.zeros((D, 2 * key_value_width), jnp.float32)
    grad_kv_weight, (grad_queries, grad_keys, grad_values) = lax.scan(
        per_tree, weight_zero,
        (queries, key_tensor, value_tensor, attention_output, output_gradient, logsumexp_rows, layer_input, parents))
    return grad_queries, grad_keys, grad_values, grad_kv_weight
```

```python
import functools

import jax
import jax.numpy as jnp
from jax import lax
from jax.experimental import pallas as pl
from jax.experimental.pallas import tpu as pltpu
from jax.sharding import PartitionSpec as P

QUERY_HEADS = 32
KEY_VALUE_HEADS = 4
HEAD_SIZE = 128
BLK = 128
GROUP = QUERY_HEADS // KEY_VALUE_HEADS
RING = 4
SIDE = 4
TREES = 8
TALL = 512
ROWS = GROUP * BLK
PACK = 2 * ROWS + 32
SCALE = HEAD_SIZE ** (-0.5)
RING_ORDER = (2, 1, 3)
LOG2E = 1.4426950408889634
F32 = jnp.float32
BF16 = jnp.bfloat16
MIB = 1 << 20


def side_perm(k):
    return [(c, c ^ k) for c in range(RING * SIDE)]


def ring_perm(s):
    return [(c, ((c // SIDE + s) % RING) * SIDE + c % SIDE) for c in range(RING * SIDE)]


def smem():
    return pl.BlockSpec(memory_space=pltpu.SMEM)


def vmem():
    return pl.BlockSpec(memory_space=pltpu.VMEM)


def call(kernel, out_shape, n_smem, n_vmem, n_any=0, scratch=(), moved=0, limit=32):
    return pl.pallas_call(
        kernel,
        out_shape=out_shape,
        in_specs=[smem()] * n_smem + [vmem()] * n_vmem + [pl.BlockSpec(memory_space=pl.ANY)] * n_any,
        out_specs=[vmem()] * len(out_shape),
        scratch_shapes=list(scratch),
        compiler_params=pltpu.CompilerParams(vmem_limit_bytes=limit * MIB),
        cost_estimate=pl.CostEstimate(flops=0, bytes_accessed=moved, transcendentals=0),
    )


def split_kv_kernel(place, key_ref, value_ref, *outs):
    own = place[1]
    for k, out in enumerate(outs):
        col = pl.multiple_of((own ^ k) * HEAD_SIZE, HEAD_SIZE)
        out[0:BLK, :] = key_ref[:, pl.ds(col, HEAD_SIZE)]
        out[BLK:, :] = value_ref[:, pl.ds(col, HEAD_SIZE)]


def split_queries_kernel(place, query_ref, gradient_ref, output_ref, lse_ref, after, *outs):
    lane = lax.broadcasted_iota(jnp.int32, (BLK, 128), 1)
    columns = jnp.zeros((BLK, 128), F32)
    for h in range(GROUP):
        cols = slice(h * HEAD_SIZE, (h + 1) * HEAD_SIZE)
        prod = gradient_ref[:, cols].astype(F32) * output_ref[:, cols].astype(F32)
        columns = jnp.where(lane == h, jnp.sum(prod, axis=1, keepdims=True), columns)
    delta = columns.T[0:GROUP]
    lse = lse_ref[...] * LOG2E

    def split(rows):
        high = rows.astype(BF16)
        low = (rows - high.astype(F32)).astype(BF16)
        return jnp.concatenate([high, low], axis=0)

    for k, out in enumerate(outs):

        @pl.when(pl.program_id(0) == k)
        def _(out=out):
            for h in range(GROUP):
                cols = slice(h * HEAD_SIZE, (h + 1) * HEAD_SIZE)
                out[h * BLK : (h + 1) * BLK, :] = query_ref[:, cols]
                out[ROWS + h * BLK : ROWS + (h + 1) * BLK, :] = gradient_ref[:, cols]
            out[2 * ROWS : 2 * ROWS + 16, :] = split(lse)
            out[2 * ROWS + 16 :, :] = split(delta)


def split_queries(place, queries, gradient, output, lse, after):
    wide = pl.BlockSpec((BLK, GROUP * HEAD_SIZE), lambda k, place: (0, place[1] ^ k))
    return pl.pallas_call(
        split_queries_kernel,
        out_shape=[shape(PACK)] * SIDE,
        grid_spec=pltpu.PrefetchScalarGridSpec(
            num_scalar_prefetch=1,
            grid=(SIDE,),
            in_specs=[
                wide,
                wide,
                wide,
                pl.BlockSpec((GROUP, BLK), lambda k, place: (place[1] ^ k, 0)),
                pl.BlockSpec(memory_space=pl.ANY),
            ],
            out_specs=[pl.BlockSpec((PACK, HEAD_SIZE), lambda k, place: (0, 0))] * SIDE,
        ),
        compiler_params=pltpu.CompilerParams(vmem_limit_bytes=56 * MIB),
        cost_estimate=pl.CostEstimate(flops=0, bytes_accessed=32 * MIB, transcendentals=0),
    )(place, queries, gradient, output, lse, after)


def ring_pack_kernel(place, inputs, *refs):
    kv, refs = refs[:SIDE], refs[SIDE + 1 :]
    outs, shares = refs[:RING], refs[RING]
    _, _, quarter = shares.shape
    piece = quarter // TREES
    for r in range(RING):
        shares[r] = jnp.concatenate(
            [inputs[:, (d * RING + r) * piece : (d * RING + r + 1) * piece] for d in range(TREES)], axis=1
        )
    for s, out in enumerate(outs):
        out[:, 0:quarter] = shares[(place[0] + s) % RING]
        for k in range(SIDE):
            for half in range(2):
                col = quarter + (2 * k + half) * HEAD_SIZE
                out[:, col : col + HEAD_SIZE] = kv[k][half * BLK : (half + 1) * BLK, :]


def attention_kernel(place, parents, *refs):
    ring_in, packs, refs = refs[:RING], refs[RING : RING + SIDE], refs[RING + SIDE + 1 :]
    dq_near, dq_far, grad_own, grad_out, refs = refs[0], refs[1], refs[2], refs[3 : RING + 2], refs[RING + 2 :]
    kv, kv_t, pack, query_t, gradient_t, col_lse, col_delta, dq_acc, dq, acc = refs
    ring, own = place[0], place[1]
    start = ring_in[0].shape[1] - 2 * SIDE * HEAD_SIZE

    for s in range(RING):
        for k in range(SIDE):
            for half in range(2):
                col = start + (2 * k + half) * HEAD_SIZE
                kv[s * SIDE + k, half * BLK : (half + 1) * BLK, :] = ring_in[s][:, col : col + HEAD_SIZE]
    for k in range(SIDE):
        pack[k] = packs[k][...]
    acc[...] = jnp.zeros_like(acc)

    @pl.loop(0, RING * SIDE)
    def _(j):
        kv_t[j, :, 0:BLK] = kv[j, 0:BLK, :].T
        kv_t[j, :, BLK:] = kv[j, BLK:, :].T

    def slot_of(at):
        return ((ring - at // SIDE) % RING) * SIDE + ((at % SIDE) ^ own)

    def tile(piece, slots, diagonal):
        n = len(slots) * BLK
        keys = jnp.concatenate([kv[j, 0:BLK, :] for j in slots], axis=0)
        keys_t = jnp.concatenate([kv_t[j, :, 0:BLK] for j in slots], axis=1)
        values_t = jnp.concatenate([kv_t[j, :, BLK:] for j in slots], axis=1)
        dk = dv = None
        for p in range(ROWS // TALL):
            span = slice(p * TALL, (p + 1) * TALL)
            scores = jnp.dot(pack[piece, span, :], keys_t, preferred_element_type=F32)
            lse = jnp.concatenate([col_lse[span, :]] * len(slots), axis=1)
            delta = jnp.concatenate([col_delta[span, :]] * len(slots), axis=1)
            prob = jnp.exp2(scores * (SCALE * LOG2E) - lse)
            if diagonal:
                query_at = lax.broadcasted_iota(jnp.int32, (TALL, n), 0) % BLK
                key_at = lax.broadcasted_iota(jnp.int32, (TALL, n), 1)
                prob = jnp.where((key_at <= query_at) | (key_at >= BLK), prob, 0.0)
            prob_grad = jnp.dot(
                pack[piece, ROWS + p * TALL : ROWS + (p + 1) * TALL, :], values_t, preferred_element_type=F32
            )
            dscore = (prob * (prob_grad - delta)).astype(BF16)
            dv_part = jnp.dot(gradient_t[:, span], prob.astype(BF16), preferred_element_type=F32)
            dk_part = jnp.dot(query_t[:, span], dscore, preferred_element_type=F32)
            dv = dv_part if dv is None else dv + dv_part
            dk = dk_part if dk is None else dk + dk_part
            part = jnp.dot(dscore, keys, preferred_element_type=F32)
            if diagonal:
                dq_acc[span, :] = part
            else:
                dq_acc[span, :] += part
        for m, j in enumerate(slots):
            acc[j, 0:BLK, :] += dk[:, m * BLK : (m + 1) * BLK]
            acc[j, BLK:, :] += dv[:, m * BLK : (m + 1) * BLK]

    @pl.loop(0, SIDE)
    def _(piece):
        terms = pack[piece, 2 * ROWS :, :].astype(F32)
        lse = terms[0:8] + terms[8:16]
        delta = terms[16:24] + terms[24:32]
        for h in range(GROUP):
            cols = slice(h * BLK, (h + 1) * BLK)
            query_t[:, cols] = pack[piece, cols, :].T
            gradient_t[:, cols] = pack[piece, ROWS + h * BLK : ROWS + (h + 1) * BLK, :].T
            col_lse[cols, :] = jnp.broadcast_to(lse[h : h + 1], (BLK, BLK)).T
            col_delta[cols, :] = jnp.broadcast_to(delta[h : h + 1], (BLK, BLK)).T

        block = ring * SIDE + (own ^ piece)
        above = lax.while_loop(lambda c: c[0] > 0, lambda c: (parents[0, c[0]], c[1] + 1), (block, 0))[1]
        odd = above % 2 == 1

        @pl.when(odd)
        def _():
            tile(piece, [piece, slot_of(parents[0, block])], True)

        @pl.when(jnp.logical_not(odd))
        def _():
            tile(piece, [piece], True)

        def ancestors(at):
            one = parents[0, at]
            two = parents[0, one]
            tile(piece, [slot_of(one), slot_of(two)], False)
            return two

        lax.while_loop(lambda at: at > 0, ancestors, jnp.where(odd, parents[0, block], block))
        dq[piece] = (dq_acc[...] * SCALE).astype(BF16)

    for k in range(SIDE):
        out = dq_near if k < 2 else dq_far
        out[(k % 2) * ROWS : (k % 2 + 1) * ROWS, :] = dq[k]
    for s in range(RING):
        for k in range(SIDE):
            dk, dv = acc[s * SIDE + k, 0:BLK, :].T * SCALE, acc[s * SIDE + k, BLK:, :].T
            out = grad_own if s == 0 else grad_out[s - 1]
            out[2 * k * BLK : (2 * k + 1) * BLK, :] = dk.astype(out.dtype)
            out[(2 * k + 1) * BLK : (2 * k + 2) * BLK, :] = dv.astype(out.dtype)


def attention_call(place, parents, ring_in, packs, after):
    sum_shape = (RING * SIDE, 2 * BLK, HEAD_SIZE)
    return call(
        attention_kernel,
        [shape(2 * ROWS)] * 2 + [shape(ROWS, kind=F32)] + [shape(ROWS)] * (RING - 1),
        2,
        RING + SIDE,
        n_any=1,
        scratch=[
            pltpu.VMEM(sum_shape, BF16),
            pltpu.VMEM((RING * SIDE, HEAD_SIZE, 2 * BLK), BF16),
            pltpu.VMEM((SIDE, PACK, HEAD_SIZE), BF16),
            pltpu.VMEM((HEAD_SIZE, ROWS), BF16),
            pltpu.VMEM((HEAD_SIZE, ROWS), BF16),
            pltpu.VMEM((ROWS, 128), F32),
            pltpu.VMEM((ROWS, 128), F32),
            pltpu.VMEM((ROWS, HEAD_SIZE), F32),
            pltpu.VMEM((SIDE, ROWS, HEAD_SIZE), BF16),
            pltpu.VMEM(sum_shape, F32),
        ],
    )(place, parents, *ring_in, *packs, after)


def total_kernel(own_ref, *refs):
    parts, total = refs[:-1], refs[-1]
    value = own_ref[...]
    for part in parts:
        value = value + part[...].astype(F32)
    total[...] = value.astype(BF16)


def relay_inputs_kernel(own, side, dq_near, dq_far, total, core_out, side_out):
    rows, cols = own.shape
    core_out[0:rows, 0:cols] = own[...]
    core_out[rows:, 0:cols] = side[...]
    core_out[:, cols:] = dq_near[ROWS:, :]
    side_out[0 : 2 * ROWS, :] = dq_far[...]
    side_out[2 * ROWS :, :] = total[4 * BLK :, :]


def relay_outputs_kernel(total, side, out):
    out[0:ROWS, :] = side[ROWS : 2 * ROWS, :]
    out[ROWS : ROWS + 2 * BLK, :] = total[2 * BLK : 4 * BLK, :]
    out[ROWS + 2 * BLK :, :] = side[2 * ROWS + 2 * BLK :, :]


def join_inputs_kernel(*refs):
    pieces, out = refs[:RING], refs[-1]
    for s in range(RING):
        out[s * BLK : (s + 1) * BLK, :] = pieces[s][:, 0 : out.shape[1]]


def projection_kernel(*refs):
    grads = dict(zip((0,) + RING_ORDER, refs[:RING]))
    own, side, core = refs[RING : RING + 3]
    out, grad_t, weight_t = refs[RING + 3 :]
    rows, cols = own.shape
    inputs = (own, core.at[0:rows, 0:cols], side, core.at[rows:, 0:cols])
    for s in range(RING):
        for k in range(SIDE):
            at = 2 * k * BLK
            grad_t[k, 0:BLK, s * BLK : (s + 1) * BLK] = grads[s][at : at + BLK, :].T
            grad_t[k, BLK:, s * BLK : (s + 1) * BLK] = grads[s][at + BLK : at + 2 * BLK, :].T
    total = jnp.dot(grad_t[0], inputs[0][...], preferred_element_type=F32)
    for k in range(1, SIDE):
        total = total + jnp.dot(grad_t[k], inputs[k][...], preferred_element_type=F32)
    weight_t[...] = total
    for n in range(out.shape[0] // BLK):
        rows = slice(n * BLK, (n + 1) * BLK)
        out[rows, 0:BLK] = weight_t[0:BLK, rows].T.astype(BF16)
        out[rows, BLK:] = weight_t[BLK:, rows].T.astype(BF16)


def join_kernel(place, near, core, side, crossed, total, queries, keys, values):
    own = place[1]
    last = core.shape[1] - HEAD_SIZE
    for h in range(GROUP):
        rows = slice(h * BLK, (h + 1) * BLK)
        for k, piece in enumerate((near[rows, :], core[rows, last:], side[rows, :], crossed[rows, :])):
            col = pl.multiple_of((own ^ k) * (GROUP * HEAD_SIZE) + h * HEAD_SIZE, HEAD_SIZE)
            queries[:, pl.ds(col, HEAD_SIZE)] = piece
    for k, (ref, at) in enumerate(((total, 0), (crossed, ROWS), (side, 2 * ROWS), (crossed, ROWS + 2 * BLK))):
        col = pl.multiple_of((own ^ k) * HEAD_SIZE, HEAD_SIZE)
        keys[:, pl.ds(col, HEAD_SIZE)] = ref[at : at + BLK, :]
        values[:, pl.ds(col, HEAD_SIZE)] = ref[at + BLK : at + 2 * BLK, :]


def shape(rows, cols=HEAD_SIZE, kind=BF16):
    return jax.ShapeDtypeStruct((rows, cols), kind)


def local(
    queries,
    key_tensor,
    value_tensor,
    attention_output,
    output_gradient,
    logsumexp_rows,
    layer_input,
    parents,
    trees,
):
    width = layer_input.shape[2]
    quarter = width // RING
    share = width // (trees * RING * SIDE)
    at = lax.axis_index("ctx")
    ring, own = at // SIDE, at % SIDE
    place = jnp.stack([ring, own]).astype(jnp.int32)

    def to_side(x, k):
        return lax.ppermute(x, "ctx", side_perm(k))

    def to_ring(x, s):
        return lax.ppermute(x, "ctx", ring_perm(s % RING))

    with jax.named_scope("keys_values"):
        kv_split = call(split_kv_kernel, [shape(2 * BLK)] * SIDE, 1, 2, limit=56)(
            place, key_tensor[0], value_tensor[0]
        )
        kv_side = [kv_split[0]] + [to_side(kv_split[k], k) for k in (1, 2, 3)]

    with jax.named_scope("queries"):
        packs = split_queries(
            place, queries[0], output_gradient[0], attention_output[0], logsumexp_rows[0], kv_split[1]
        )
        packs = [packs[0]] + [to_side(packs[k], k) for k in (1, 2, 3)]

    with jax.named_scope("ring"):
        ring_out = call(
            ring_pack_kernel,
            [shape(BLK, quarter + 2 * SIDE * HEAD_SIZE)] * RING,
            1,
            1 + SIDE,
            n_any=1,
            moved=16 * MIB,
            scratch=[pltpu.VMEM((RING, BLK, quarter), BF16)],
        )(place, layer_input[0], *kv_side, packs[1])
        ring_in = {s: to_ring(ring_out[s], s) for s in RING_ORDER}
        ring_in = [ring_out[0]] + [ring_in[s] for s in (1, 2, 3)]

    with jax.named_scope("inputs_side"):
        input_own = call(join_inputs_kernel, [shape(RING * BLK, quarter)], 0, RING, n_any=3)(
            *ring_in, *packs[1:]
        )[0]
        input_y = to_side(input_own, 2)

    with jax.named_scope("attention"):
        outs = attention_call(place, parents, ring_in, packs, input_own)
        dq_near, dq_far, grad_own, grad_parts = outs[0], outs[1], outs[2], outs[3:]

    with jax.named_scope("kv_gradients"):
        received = [to_ring(grad_parts[s - 1], -s) for s in RING_ORDER]
        grad_total = call(total_kernel, [shape(ROWS)], 0, RING)(grad_own, *received)[0]
        grads = [grad_total] + [to_ring(grad_total, s) for s in RING_ORDER]

    with jax.named_scope("to_core"):
        core_out, side_out = call(
            relay_inputs_kernel,
            [shape(2 * RING * BLK, quarter + HEAD_SIZE), shape(2 * ROWS + 4 * BLK)],
            0,
            5,
        )(input_own, input_y, dq_near, dq_far, grad_total)
        core = to_side(core_out, 1)

    with jax.named_scope("own_gradients"):
        side = to_side(side_out, 2)
        crossed = to_side(call(relay_outputs_kernel, [shape(ROWS + 4 * BLK)], 0, 2)(grad_total, side)[0], 1)
        grad_queries, grad_keys, grad_values = call(
            join_kernel,
            [shape(BLK, QUERY_HEADS * HEAD_SIZE)] + [shape(BLK, KEY_VALUE_HEADS * HEAD_SIZE)] * 2,
            1,
            5,
        )(place, dq_near, core, side, crossed, grad_total)

    with jax.named_scope("projection"):
        partial = call(
            projection_kernel,
            [shape(quarter, 2 * HEAD_SIZE)],
            0,
            RING + 3,
            scratch=[
                pltpu.VMEM((SIDE, 2 * BLK, RING * BLK), BF16),
                pltpu.VMEM((2 * BLK, quarter), F32),
            ],
        )(*grads, input_own, input_y, core)[0]

    with jax.named_scope("projection_sum"):
        groups = [
            [d * RING * SIDE + r * SIDE + g for d in range(trees) for g in range(SIDE)]
            for r in range(RING)
        ]
        swapped = lax.all_to_all(
            partial.reshape(trees * SIDE, share, 2 * HEAD_SIZE),
            ("dp", "ctx"),
            0,
            0,
            axis_index_groups=groups,
            tiled=True,
        )
        summed = jnp.sum(swapped.reshape(trees, SIDE, share, 2, HEAD_SIZE).astype(F32), axis=0)
        grad_kv_weight = summed.transpose(1, 2, 0, 3).reshape(share, 2 * KEY_VALUE_HEADS * HEAD_SIZE)

    return grad_queries[None], grad_keys[None], grad_values[None], grad_kv_weight


def solution(mesh):
    in_specs = (
        P("dp", "ctx", None),
        P("dp", "ctx", None),
        P("dp", "ctx", None),
        P("dp", "ctx", None),
        P("dp", "ctx", None),
        P("dp", None, "ctx"),
        P("dp", "ctx", None),
        P("dp", None),
    )
    out_specs = (
        P("dp", "ctx", None),
        P("dp", "ctx", None),
        P("dp", "ctx", None),
        P(("dp", "ctx"), None),
    )
    return jax.shard_map(
        functools.partial(local, trees=mesh.shape["dp"]),
        mesh=mesh,
        in_specs=in_specs,
        out_specs=out_specs,
        check_vma=False,
    )
```

```python
import functools

import jax
import jax.numpy as jnp
from jax import lax
from jax.experimental import pallas as pl
from jax.experimental.pallas import tpu as pltpu
from jax.sharding import PartitionSpec as P

QUERY_HEADS = 32
KEY_VALUE_HEADS = 4
HEAD_SIZE = 128
BLK = 128
GROUP = QUERY_HEADS // KEY_VALUE_HEADS
RING = 4
SIDE = 4
TREES = 8
TALL = 1024
ROWS = GROUP * BLK
PACK = 2 * ROWS + 272
SCALE = HEAD_SIZE ** (-0.5)
RING_ORDER = (2, 1, 3)
LOG2E = 1.4426950408889634
LSE_SCALE = HEAD_SIZE**0.5
F32 = jnp.float32
BF16 = jnp.bfloat16
MIB = 1 << 20


def side_perm(k):
    return [(c, c ^ k) for c in range(RING * SIDE)]


def ring_perm(s):
    return [(c, ((c // SIDE + s) % RING) * SIDE + c % SIDE) for c in range(RING * SIDE)]


def smem():
    return pl.BlockSpec(memory_space=pltpu.SMEM)


def vmem():
    return pl.BlockSpec(memory_space=pltpu.VMEM)


def call(kernel, out_shape, n_smem, n_vmem, n_any=0, scratch=(), moved=0, limit=20):
    return pl.pallas_call(
        kernel,
        out_shape=out_shape,
        in_specs=[smem()] * n_smem + [vmem()] * n_vmem + [pl.BlockSpec(memory_space=pl.ANY)] * n_any,
        out_specs=[vmem()] * len(out_shape),
        scratch_shapes=list(scratch),
        compiler_params=pltpu.CompilerParams(vmem_limit_bytes=limit * MIB),
        cost_estimate=pl.CostEstimate(flops=0, bytes_accessed=moved, transcendentals=0),
    )


def split_kv_kernel(place, key_ref, value_ref, *outs):
    own = place[1]
    for k, out in enumerate(outs):
        col = pl.multiple_of((own ^ k) * HEAD_SIZE, HEAD_SIZE)
        out[0:BLK, :] = key_ref[:, pl.ds(col, HEAD_SIZE)]
        out[BLK:, :] = value_ref[:, pl.ds(col, HEAD_SIZE)]


def split_queries_kernel(place, query_ref, gradient_ref, output_ref, lse_ref, after, *outs):
    lane = lax.broadcasted_iota(jnp.int32, (BLK, 128), 1)
    columns = jnp.zeros((BLK, 128), F32)
    for h in range(GROUP):
        cols = slice(h * HEAD_SIZE, (h + 1) * HEAD_SIZE)
        prod = gradient_ref[:, cols].astype(F32) * output_ref[:, cols].astype(F32)
        columns = jnp.where(lane == h, jnp.sum(prod, axis=1, keepdims=True), columns)
    delta = columns.T[0:GROUP]
    lse = lse_ref[...] * LSE_SCALE

    def split(rows):
        high = rows.astype(BF16)
        low = (rows - high.astype(F32)).astype(BF16)
        return jnp.concatenate([high, low], axis=0)

    for k, out in enumerate(outs):

        @pl.when(pl.program_id(0) == k)
        def _(out=out):
            for h in range(GROUP):
                cols = slice(h * HEAD_SIZE, (h + 1) * HEAD_SIZE)
                out[h * BLK : (h + 1) * BLK, :] = query_ref[:, cols]
                out[ROWS + h * BLK : ROWS + (h + 1) * BLK, :] = gradient_ref[:, cols]
            out[2 * ROWS : 2 * ROWS + 16, :] = split(lse)
            out[2 * ROWS + 16 : 2 * ROWS + 32, :] = split(delta)


def split_queries(place, queries, gradient, output, lse, after, first):
    count = SIDE // 2
    wide = pl.BlockSpec((BLK, GROUP * HEAD_SIZE), lambda k, place: (0, place[1] ^ (first + k)))
    return pl.pallas_call(
        split_queries_kernel,
        out_shape=[shape(PACK)] * count,
        grid_spec=pltpu.PrefetchScalarGridSpec(
            num_scalar_prefetch=1,
            grid=(count,),
            in_specs=[
                wide,
                wide,
                wide,
                pl.BlockSpec((GROUP, BLK), lambda k, place: (place[1] ^ (first + k), 0)),
                pl.BlockSpec(memory_space=pl.ANY),
            ],
            out_specs=[pl.BlockSpec((PACK, HEAD_SIZE), lambda k, place: (0, 0))] * count,
        ),
        compiler_params=pltpu.CompilerParams(vmem_limit_bytes=56 * MIB),
        cost_estimate=pl.CostEstimate(flops=0, bytes_accessed=32 * MIB, transcendentals=0),
    )(place, queries, gradient, output, lse, after)


def ring_pack_kernel(place, inputs, *refs):
    kv, refs = refs[:SIDE], refs[SIDE + 1 :]
    outs, token, shares = refs[:RING], refs[RING], refs[RING + 1]
    token[...] = jnp.zeros_like(token)
    _, _, quarter = shares.shape
    piece = quarter // TREES
    for r in range(RING):
        shares[r] = jnp.concatenate(
            [inputs[:, (d * RING + r) * piece : (d * RING + r + 1) * piece] for d in range(TREES)], axis=1
        )
    for s, out in enumerate(outs):
        out[:, 0:quarter] = shares[(place[0] + s) % RING]
        for k in range(SIDE):
            for half in range(2):
                col = quarter + (2 * k + half) * HEAD_SIZE
                out[:, col : col + HEAD_SIZE] = kv[k][half * BLK : (half + 1) * BLK, :]


def attention_kernel(place, parents, *refs):
    ring_in, packs, refs = refs[:RING], refs[RING : RING + SIDE], refs[RING + SIDE + 1 :]
    dq_outs, grad_outs, refs = refs[:2], refs[2 : 2 + RING], refs[2 + RING :]
    kv, kv_t, pack, query_t, gradient_t, terms, dq_acc, dq, acc, stage_own, stage, kv_sem, pack_sem, out_sem = refs
    ring, own = place[0], place[1]
    start = ring_in[0].shape[1] - 2 * SIDE * HEAD_SIZE

    loads = []
    for s in range(RING):
        for k in range(SIDE):
            for half in range(2):
                col = start + (2 * k + half) * HEAD_SIZE
                loads.append(
                    pltpu.make_async_copy(
                        ring_in[s].at[:, pl.ds(col, HEAD_SIZE)],
                        kv.at[s * SIDE + k, pl.ds(half * BLK, BLK), :],
                        kv_sem.at[len(loads)],
                    )
                )
    pack_loads = [pltpu.make_async_copy(packs[k], pack.at[k], pack_sem.at[k]) for k in range(SIDE)]
    for load in loads + pack_loads:
        load.start()
    acc[...] = jnp.zeros_like(acc)
    for load in loads:
        load.wait()

    row = lax.broadcasted_iota(jnp.int32, (BLK, BLK), 0)
    minus_lse = jnp.where(row < 16, -1.0, 0.0).astype(BF16)
    minus_delta = jnp.where((row >= 16) & (row < 32), -1.0, 0.0).astype(BF16)

    @pl.loop(0, RING * SIDE // 4)
    def _(quarter):
        for part in range(4):
            j = quarter * 4 + part
            kv_t[j, 0:BLK, 0:BLK] = kv[j, 0:BLK, :].T
            kv_t[j, 0:BLK, BLK:] = kv[j, BLK:, :].T
            kv_t[j, BLK:, 0:BLK] = minus_lse
            kv_t[j, BLK:, BLK:] = minus_delta

    for load in pack_loads:
        load.wait()

    def store_dq(k):
        place_out = dq_outs[k // 2].at[pl.ds(k % 2 * ROWS, ROWS), :]
        return pltpu.make_async_copy(dq.at[k], place_out, out_sem.at[k])

    def slot_of(at):
        return ((ring - at // SIDE) % RING) * SIDE + ((at % SIDE) ^ own)

    def tile(piece, slots, diagonal):
        n = len(slots) * BLK
        keys = jnp.concatenate([kv[j, 0:BLK, :] for j in slots], axis=0)
        keys_t = jnp.concatenate([kv_t[j, :, 0:BLK] for j in slots], axis=1)
        values_t = jnp.concatenate([kv_t[j, :, BLK:] for j in slots], axis=1)
        dk = dv = None
        for p in range(ROWS // TALL):
            span = slice(p * TALL, (p + 1) * TALL)
            extra = terms[span, :]
            scores = jnp.dot(
                jnp.concatenate([pack[piece, span, :], extra], axis=1), keys_t, preferred_element_type=F32
            )
            prob = jnp.exp2(scores * (SCALE * LOG2E))
            if diagonal:
                query_at = lax.broadcasted_iota(jnp.int32, (TALL, n), 0) % BLK
                key_at = lax.broadcasted_iota(jnp.int32, (TALL, n), 1)
                prob = jnp.where((key_at <= query_at) | (key_at >= BLK), prob, 0.0)
            prob_grad = jnp.dot(
                jnp.concatenate([pack[piece, ROWS + p * TALL : ROWS + (p + 1) * TALL, :], extra], axis=1),
                values_t,
                preferred_element_type=F32,
            )
            dscore = (prob * prob_grad).astype(BF16)
            dv_part = jnp.dot(gradient_t[:, span], prob.astype(BF16), preferred_element_type=F32)
            dk_part = jnp.dot(query_t[:, span], dscore, preferred_element_type=F32)
            dv = dv_part if dv is None else dv + dv_part
            dk = dk_part if dk is None else dk + dk_part
            part = jnp.dot(dscore, keys, preferred_element_type=F32)
            if diagonal:
                dq_acc[span, :] = part
            else:
                dq_acc[span, :] += part
        for m, j in enumerate(slots):
            acc[j, 0:BLK, :] += dk[:, m * BLK : (m + 1) * BLK]
            acc[j, BLK:, :] += dv[:, m * BLK : (m + 1) * BLK]

    @pl.loop(0, SIDE)
    def _(piece):
        lane = lax.broadcasted_iota(jnp.int32, (BLK, 128), 1)
        columns = jnp.concatenate(
            [pack[piece, 2 * ROWS : 2 * ROWS + 32, :].astype(F32), jnp.zeros((BLK - 32, BLK), F32)], axis=0
        ).T
        for h in range(GROUP):
            cols = slice(h * BLK, (h + 1) * BLK)
            query_t[:, cols] = pack[piece, cols, :].T
            gradient_t[:, cols] = pack[piece, ROWS + h * BLK : ROWS + (h + 1) * BLK, :].T
            terms[cols, :] = jnp.where(lane % GROUP == h, columns, 0.0).astype(BF16)

        block = ring * SIDE + (own ^ piece)
        above = lax.while_loop(lambda c: c[0] > 0, lambda c: (parents[0, c[0]], c[1] + 1), (block, 0))[1]
        odd = above % 2 == 1

        @pl.when(odd)
        def _():
            tile(piece, [piece, slot_of(parents[0, block])], True)

        @pl.when(jnp.logical_not(odd))
        def _():
            tile(piece, [piece], True)

        def ancestors(at):
            one = parents[0, at]
            two = parents[0, one]
            tile(piece, [slot_of(one), slot_of(two)], False)
            return two

        def quad(c):
            at, left = c
            one = parents[0, at]
            two = parents[0, one]
            three = parents[0, two]
            four = parents[0, three]
            tile(piece, [slot_of(one), slot_of(two), slot_of(three), slot_of(four)], False)
            return four, left - 4

        start = jnp.where(odd, parents[0, block], block)
        at, left = lax.while_loop(lambda c: c[1] >= 4, quad, (start, above - odd.astype(jnp.int32)))

        @pl.when(left > 0)
        def _():
            ancestors(at)

        dq[piece] = (dq_acc[...] * SCALE).astype(BF16)
        for k in range(SIDE):

            @pl.when(piece == k)
            def _(k=k):
                store_dq(k).start()

    stores = [store_dq(k) for k in range(SIDE)]
    for s in RING_ORDER + (0,):
        for k in range(SIDE):
            dk, dv = acc[s * SIDE + k, 0:BLK, :] * SCALE, acc[s * SIDE + k, BLK:, :]
            at = 2 * k * BLK
            if s == 0:
                stage_own[at : at + BLK, :] = dk.T
                stage_own[at + BLK : at + 2 * BLK, :] = dv.T
            else:
                stage[s - 1, at : at + BLK, :] = dk.astype(BF16).T
                stage[s - 1, at + BLK : at + 2 * BLK, :] = dv.astype(BF16).T
        source = stage_own if s == 0 else stage.at[s - 1]
        stores.append(pltpu.make_async_copy(source, grad_outs[s], out_sem.at[SIDE + s]))
        stores[-1].start()
    for store in stores:
        store.wait()


def attention_call(place, parents, ring_in, packs, *after):
    sum_shape = (RING * SIDE, 2 * BLK, HEAD_SIZE)
    hbm = pl.BlockSpec(memory_space=pl.ANY)
    return pl.pallas_call(
        attention_kernel,
        out_shape=[shape(2 * ROWS), shape(2 * ROWS + 4 * BLK), shape(ROWS, kind=F32)]
        + [shape(ROWS)] * (RING - 1),
        in_specs=[smem()] * 2 + [hbm] * (RING + SIDE + 1),
        out_specs=[hbm] * (2 + RING),
        scratch_shapes=[
            pltpu.VMEM(sum_shape, BF16),
            pltpu.VMEM((RING * SIDE, 2 * HEAD_SIZE, 2 * BLK), BF16),
            pltpu.VMEM((SIDE, PACK, HEAD_SIZE), BF16),
            pltpu.VMEM((HEAD_SIZE, ROWS), BF16),
            pltpu.VMEM((HEAD_SIZE, ROWS), BF16),
            pltpu.VMEM((ROWS, 128), BF16),
            pltpu.VMEM((ROWS, HEAD_SIZE), F32),
            pltpu.VMEM((SIDE, ROWS, HEAD_SIZE), BF16),
            pltpu.VMEM(sum_shape, F32),
            pltpu.VMEM((ROWS, HEAD_SIZE), F32),
            pltpu.VMEM((RING - 1, ROWS, HEAD_SIZE), BF16),
            pltpu.SemaphoreType.DMA((2 * RING * SIDE,)),
            pltpu.SemaphoreType.DMA((SIDE,)),
            pltpu.SemaphoreType.DMA((SIDE + RING,)),
        ],
        compiler_params=pltpu.CompilerParams(vmem_limit_bytes=24 * MIB),
        cost_estimate=pl.CostEstimate(flops=0, bytes_accessed=0, transcendentals=0),
    )(place, parents, *ring_in, *packs, *after)


def total_kernel(grad_own, *refs):
    parts, (total, _, side, sem) = refs[: RING - 1], refs[RING + 2 :]
    value = grad_own[...]
    for part in parts:
        value = value + part[...].astype(F32)
    total[...] = value.astype(BF16)
    store = pltpu.make_async_copy(
        total.at[pl.ds(4 * BLK, 4 * BLK), :], side.at[pl.ds(2 * ROWS, 4 * BLK), :], sem
    )
    store.start()
    store.wait()


def total_call(grad_own, received, inputs, side, after):
    hbm = pl.BlockSpec(memory_space=pl.ANY)
    return pl.pallas_call(
        total_kernel,
        out_shape=[shape(ROWS), shape(*inputs.shape), shape(*side.shape)],
        in_specs=[vmem()] * RING + [hbm] * 3,
        out_specs=[vmem(), hbm, hbm],
        scratch_shapes=[pltpu.SemaphoreType.DMA],
        input_output_aliases={RING: 1, RING + 1: 2},
        compiler_params=pltpu.CompilerParams(vmem_limit_bytes=16 * MIB),
        cost_estimate=pl.CostEstimate(flops=0, bytes_accessed=0, transcendentals=0),
    )(grad_own, *received, inputs, side, after)


def relay_kernel(near, side, total, *rest):
    out = rest[-1]
    out[0:ROWS, :] = side[ROWS : 2 * ROWS, :]
    out[ROWS : ROWS + 2 * BLK, :] = total[2 * BLK : 4 * BLK, :]
    out[ROWS + 2 * BLK : ROWS + 4 * BLK, :] = side[2 * ROWS + 2 * BLK :, :]
    out[ROWS + 4 * BLK :, :] = near[ROWS:, :]


def join_inputs_kernel(*refs):
    pieces, out = refs[:RING], refs[-1]
    for s in range(RING):
        out[s * BLK : (s + 1) * BLK, :] = pieces[s][:, 0 : out.shape[1]]


def projection_kernel(*refs):
    grads = dict(zip((0,) + RING_ORDER, refs[:RING]))
    inputs = refs[RING : RING + SIDE]
    out, grad_t, weight_t, keys, values = refs[RING + SIDE :]
    for s in range(RING):
        for k in range(SIDE):
            at = 2 * k * BLK
            grad_t[k, 0:BLK, s * BLK : (s + 1) * BLK] = grads[s][at : at + BLK, :].T
            grad_t[k, BLK:, s * BLK : (s + 1) * BLK] = grads[s][at + BLK : at + 2 * BLK, :].T
    total = jnp.dot(grad_t[0], inputs[0][...], preferred_element_type=F32)
    for k in range(1, SIDE):
        total = total + jnp.dot(grad_t[k], inputs[k][...], preferred_element_type=F32)
    weight_t[...] = total
    for n in range(keys.shape[0] // BLK):
        rows = slice(n * BLK, (n + 1) * BLK)
        keys[rows, :] = weight_t[0:BLK, rows].T
        values[rows, :] = weight_t[BLK:, rows].T
    count, both, _ = out.shape
    for j in range(count):
        rows = slice(j * (both // 2), (j + 1) * (both // 2))
        out[j] = jnp.concatenate([keys[rows, :], values[rows, :]], axis=0).astype(BF16)


def weight_kernel(parts, out):
    share = out.shape[0]
    for g in range(KEY_VALUE_HEADS):
        total = parts[g].astype(F32)
        for d in range(1, TREES):
            total = total + parts[d * SIDE + g].astype(F32)
        out[:, g * HEAD_SIZE : (g + 1) * HEAD_SIZE] = total[0:share]
        col = (KEY_VALUE_HEADS + g) * HEAD_SIZE
        out[:, col : col + HEAD_SIZE] = total[share:]


def join_kernel(place, near, side, crossed, total, queries, keys, values):
    own = place[1]
    kv_at = ROWS + 4 * BLK
    for h in range(GROUP):
        rows = slice(h * BLK, (h + 1) * BLK)
        last = slice(kv_at + h * BLK, kv_at + (h + 1) * BLK)
        for k, piece in enumerate((near[rows, :], crossed[last, :], side[rows, :], crossed[rows, :])):
            col = pl.multiple_of((own ^ k) * (GROUP * HEAD_SIZE) + h * HEAD_SIZE, HEAD_SIZE)
            queries[:, pl.ds(col, HEAD_SIZE)] = piece
    for k, (ref, at) in enumerate(((total, 0), (crossed, ROWS), (side, 2 * ROWS), (crossed, ROWS + 2 * BLK))):
        col = pl.multiple_of((own ^ k) * HEAD_SIZE, HEAD_SIZE)
        keys[:, pl.ds(col, HEAD_SIZE)] = ref[at : at + BLK, :]
        values[:, pl.ds(col, HEAD_SIZE)] = ref[at + BLK : at + 2 * BLK, :]


def shape(rows, cols=HEAD_SIZE, kind=BF16):
    return jax.ShapeDtypeStruct((rows, cols), kind)


def local(
    queries,
    key_tensor,
    value_tensor,
    attention_output,
    output_gradient,
    logsumexp_rows,
    layer_input,
    parents,
    trees,
):
    width = layer_input.shape[2]
    quarter = width // RING
    share = width // (trees * RING * SIDE)
    at = lax.axis_index("ctx")
    ring, own = at // SIDE, at % SIDE
    place = jnp.stack([ring, own]).astype(jnp.int32)

    def to_side(x, k):
        return lax.ppermute(x, "ctx", side_perm(k))

    def to_ring(x, s):
        return lax.ppermute(x, "ctx", ring_perm(s % RING))

    with jax.named_scope("keys_values"):
        kv_split = call(split_kv_kernel, [shape(2 * BLK)] * SIDE, 1, 2, limit=56)(
            place, key_tensor[0], value_tensor[0]
        )
        kv_side = [kv_split[0]] + [to_side(kv_split[k], k) for k in (1, 2, 3)]

    query_args = (queries[0], output_gradient[0], attention_output[0], logsumexp_rows[0])
    with jax.named_scope("queries_far"):
        far_own = split_queries(place, *query_args, kv_split[1], 2)
        packs_far = [to_side(far_own[k - 2], k) for k in (2, 3)]

    with jax.named_scope("ring"):
        ring_out = call(
            ring_pack_kernel,
            [shape(BLK, quarter + 2 * SIDE * HEAD_SIZE)] * RING + [shape(8, 128, F32)],
            1,
            1 + SIDE,
            n_any=1,
            moved=128 * MIB,
            scratch=[pltpu.VMEM((RING, BLK, quarter), BF16)],
        )(place, layer_input[0], *kv_side, far_own[0])
        ring_in = {s: to_ring(ring_out[s], s) for s in RING_ORDER}
        ring_in = [ring_out[0]] + [ring_in[s] for s in (1, 2, 3)]

    with jax.named_scope("queries_near"):
        near_own = split_queries(place, *query_args, ring_out[RING], 0)
        packs = [near_own[0], to_side(near_own[1], 1)] + packs_far

    with jax.named_scope("inputs_side"):
        input_own = call(join_inputs_kernel, [shape(RING * BLK, quarter)], 0, RING, n_any=3)(
            *ring_in, *packs_far, near_own[0]
        )[0]
        input_y = to_side(input_own, 2)
        input_core = to_side(input_own, 1)

    with jax.named_scope("attention"):
        outs = attention_call(place, parents, ring_in, packs, input_own)
        dq_near, side_out, grad_own, grad_parts = outs[0], outs[1], outs[2], outs[3:]

    with jax.named_scope("kv_gradients"):
        received = [to_ring(grad_parts[s - 1], -s) for s in RING_ORDER]
        grad_total, input_y, side_out = total_call(grad_own, received, input_y, side_out, input_core)
        input_last = to_side(input_y, 1)
        grads = [grad_total] + [to_ring(grad_total, s) for s in RING_ORDER]

    with jax.named_scope("projection"):
        partial = call(
            projection_kernel,
            [jax.ShapeDtypeStruct((trees * SIDE, 2 * share, HEAD_SIZE), BF16)],
            0,
            RING + SIDE,
            scratch=[
                pltpu.VMEM((SIDE, 2 * BLK, RING * BLK), BF16),
                pltpu.VMEM((2 * BLK, quarter), F32),
                pltpu.VMEM((quarter, HEAD_SIZE), F32),
                pltpu.VMEM((quarter, HEAD_SIZE), F32),
            ],
        )(*grads, input_own, input_core, input_y, input_last)[0]

    with jax.named_scope("own_gradients"):
        side = to_side(side_out, 2)
        crossed = to_side(
            call(relay_kernel, [shape(2 * ROWS + 4 * BLK)], 0, 3, n_any=3)(dq_near, side, grad_total, *grads[1:])[0], 1
        )
        grad_queries, grad_keys, grad_values = call(
            join_kernel,
            [shape(BLK, QUERY_HEADS * HEAD_SIZE)] + [shape(BLK, KEY_VALUE_HEADS * HEAD_SIZE)] * 2,
            1,
            4,
            moved=64 * MIB,
        )(place, dq_near, side, crossed, grad_total)

    with jax.named_scope("projection_sum"):
        groups = [
            [d * RING * SIDE + r * SIDE + g for d in range(trees) for g in range(SIDE)]
            for r in range(RING)
        ]
        swapped = lax.all_to_all(partial, ("dp", "ctx"), 0, 0, axis_index_groups=groups, tiled=True)
        grad_kv_weight = call(weight_kernel, [shape(share, 2 * KEY_VALUE_HEADS * HEAD_SIZE, F32)], 0, 1)(swapped)[0]

    return grad_queries[None], grad_keys[None], grad_values[None], grad_kv_weight


def solution(mesh):
    in_specs = (
        P("dp", "ctx", None),
        P("dp", "ctx", None),
        P("dp", "ctx", None),
        P("dp", "ctx", None),
        P("dp", "ctx", None),
        P("dp", None, "ctx"),
        P("dp", "ctx", None),
        P("dp", None),
    )
    out_specs = (
        P("dp", "ctx", None),
        P("dp", "ctx", None),
        P("dp", "ctx", None),
        P(("dp", "ctx"), None),
    )
    return jax.shard_map(
        functools.partial(local, trees=mesh.shape["dp"]),
        mesh=mesh,
        in_specs=in_specs,
        out_specs=out_specs,
        check_vma=False,
    )
```

```python
import functools

import jax
import jax.numpy as jnp
from jax import lax
from jax.experimental import pallas as pl
from jax.experimental.pallas import tpu as pltpu
from jax.sharding import PartitionSpec as P

QUERY_HEADS = 32
KEY_VALUE_HEADS = 4
HEAD_SIZE = 128
BLK = 128
GROUP = QUERY_HEADS // KEY_VALUE_HEADS
RING = 4
SIDE = 4
TREES = 8
PAIR = 2
TALL = 1024
ROWS = GROUP * BLK
PACK = 2 * ROWS + 32
SCALE = HEAD_SIZE ** (-0.5)
RING_ORDER = (2, 1, 3)
LOG2E = 1.4426950408889634
LSE_SCALE = HEAD_SIZE**0.5
F32 = jnp.float32
BF16 = jnp.bfloat16
MIB = 1 << 20


def side_perm(k):
    return [(c, c ^ k) for c in range(RING * SIDE)]


def ring_perm(s):
    return [(c, ((c // SIDE + s) % RING) * SIDE + c % SIDE) for c in range(RING * SIDE)]


def smem():
    return pl.BlockSpec(memory_space=pltpu.SMEM)


def vmem():
    return pl.BlockSpec(memory_space=pltpu.VMEM)


def call(kernel, out_shape, n_smem, n_vmem, n_any=0, scratch=(), moved=0, limit=20):
    return pl.pallas_call(
        kernel,
        out_shape=out_shape,
        in_specs=[smem()] * n_smem + [vmem()] * n_vmem + [pl.BlockSpec(memory_space=pl.ANY)] * n_any,
        out_specs=[vmem()] * len(out_shape),
        scratch_shapes=list(scratch),
        compiler_params=pltpu.CompilerParams(vmem_limit_bytes=limit * MIB),
        cost_estimate=pl.CostEstimate(flops=0, bytes_accessed=moved, transcendentals=0),
    )


def split_kv_kernel(place, key_ref, value_ref, *outs):
    own = place[1]
    for k, out in enumerate(outs):
        col = pl.multiple_of((own ^ k) * HEAD_SIZE, HEAD_SIZE)
        out[0:BLK, :] = key_ref[:, pl.ds(col, HEAD_SIZE)]
        out[BLK:, :] = value_ref[:, pl.ds(col, HEAD_SIZE)]


def split_queries_kernel(place, query_ref, gradient_ref, output_ref, lse_ref, kv_ref, after, *outs):
    outs, token = outs[:-1], outs[-1]
    token[...] = jnp.zeros_like(token)
    lane = lax.broadcasted_iota(jnp.int32, (BLK, 128), 1)
    columns = jnp.zeros((BLK, 128), F32)
    for h in range(GROUP):
        cols = slice(h * HEAD_SIZE, (h + 1) * HEAD_SIZE)
        prod = gradient_ref[:, cols].astype(F32) * output_ref[:, cols].astype(F32)
        columns = jnp.where(lane == h, jnp.sum(prod, axis=1, keepdims=True), columns)
    delta = columns.T[0:GROUP]
    lse = lse_ref[...] * LSE_SCALE

    def split(rows):
        high = rows.astype(BF16)
        low = (rows - high.astype(F32)).astype(BF16)
        return jnp.concatenate([high, low], axis=0)

    for k, out in enumerate(outs):

        @pl.when(pl.program_id(0) == k)
        def _(out=out):
            for h in range(GROUP):
                cols = slice(h * HEAD_SIZE, (h + 1) * HEAD_SIZE)
                out[h * BLK : (h + 1) * BLK, :] = query_ref[:, cols]
                out[ROWS + h * BLK : ROWS + (h + 1) * BLK, :] = gradient_ref[:, cols]
            out[2 * ROWS : 2 * ROWS + 16, :] = split(lse)
            out[2 * ROWS + 16 : 2 * ROWS + 32, :] = split(delta)
            if out.shape[0] > PACK:
                out[PACK:, :] = kv_ref[...]


def split_queries(place, queries, gradient, output, lse, kv, after, first):
    count = SIDE // 2
    rows = PACK if first else PACK + 2 * BLK
    wide = pl.BlockSpec((BLK, GROUP * HEAD_SIZE), lambda k, place: (0, place[1] ^ (first + k)))
    return pl.pallas_call(
        split_queries_kernel,
        out_shape=[shape(rows)] * count + [shape(8, 128, F32)],
        grid_spec=pltpu.PrefetchScalarGridSpec(
            num_scalar_prefetch=1,
            grid=(count,),
            in_specs=[
                wide,
                wide,
                wide,
                pl.BlockSpec((GROUP, BLK), lambda k, place: (place[1] ^ (first + k), 0)),
                pl.BlockSpec((2 * BLK, HEAD_SIZE), lambda k, place: (0, 0)),
                pl.BlockSpec(memory_space=pl.ANY),
            ],
            out_specs=[pl.BlockSpec((rows, HEAD_SIZE), lambda k, place: (0, 0))] * count
            + [pl.BlockSpec((8, 128), lambda k, place: (0, 0))],
        ),
        compiler_params=pltpu.CompilerParams(vmem_limit_bytes=56 * MIB),
        cost_estimate=pl.CostEstimate(flops=0, bytes_accessed=32 * MIB, transcendentals=0),
    )(place, queries, gradient, output, lse, kv, after)


def stack_kernel(*refs):
    out, token = refs[-2:]
    token[...] = jnp.zeros_like(token)
    rows = refs[0].shape[0]
    for k in range(SIDE):
        out[k * rows : (k + 1) * rows, :] = refs[k][refs[k].shape[0] - rows :, :]


def share_inputs_kernel(place, inputs, *refs):
    outs, shares = refs[-1 - RING : -1], refs[-1]
    _, _, quarter = shares.shape
    piece = quarter // TREES
    for r in range(RING):
        shares[r] = jnp.concatenate(
            [inputs[:, (d * RING + r) * piece : (d * RING + r + 1) * piece] for d in range(TREES)], axis=1
        )
    for s, out in enumerate(outs):
        out[...] = shares[(place[0] + s) % RING]


def attention_kernel(first, place, parents, *refs):
    last = first > 0
    kv_in, packs, refs = refs[:RING], refs[RING : RING + PAIR], refs[RING + PAIR :]
    if last:
        sums_in, dq_out, grad_outs, refs = refs[0], refs[2], refs[3 : 3 + RING], refs[3 + RING :]
    else:
        dq_out, sums_out, refs = refs[0], refs[1], refs[2:]
    kv, kv_t, pack, query_t, gradient_t, terms, dq_acc, dq, acc, stage_own, stage, kv_sem, pack_sem, out_sem = refs
    ring, own = place[0], place[1]

    loads = []
    for s in range(RING):
        for k in range(SIDE):
            slot = s * SIDE + k
            source = kv_in[s].at[pl.ds(2 * k * BLK, 2 * BLK), :]
            loads.append(pltpu.make_async_copy(source, kv.at[slot], kv_sem.at[slot]))
    pack_loads = [
        pltpu.make_async_copy(packs[k].at[pl.ds(0, PACK), :], pack.at[k], pack_sem.at[k]) for k in range(PAIR)
    ]
    if last:
        pack_loads.append(pltpu.make_async_copy(sums_in, acc, pack_sem.at[PAIR]))
    for load in loads + pack_loads:
        load.start()
    if not last:
        acc[...] = jnp.zeros_like(acc)
    for load in loads:
        load.wait()

    row = lax.broadcasted_iota(jnp.int32, (BLK, BLK), 0)
    minus_lse = jnp.where(row < 16, -1.0, 0.0).astype(BF16)
    minus_delta = jnp.where((row >= 16) & (row < 32), -1.0, 0.0).astype(BF16)

    @pl.loop(0, RING * SIDE // 4)
    def _(quarter):
        for part in range(4):
            j = quarter * 4 + part
            kv_t[j, 0:BLK, 0:BLK] = kv[j, 0:BLK, :].T
            kv_t[j, 0:BLK, BLK:] = kv[j, BLK:, :].T
            kv_t[j, BLK:, 0:BLK] = minus_lse
            kv_t[j, BLK:, BLK:] = minus_delta

    for load in pack_loads:
        load.wait()

    def store_dq(k):
        return pltpu.make_async_copy(dq.at[k], dq_out.at[pl.ds(k * ROWS, ROWS), :], out_sem.at[k])

    def slot_of(at):
        return ((ring - at // SIDE) % RING) * SIDE + ((at % SIDE) ^ own)

    def tile(piece, slots, diagonal):
        n = len(slots) * BLK
        keys = jnp.concatenate([kv[j, 0:BLK, :] for j in slots], axis=0)
        keys_t = jnp.concatenate([kv_t[j, :, 0:BLK] for j in slots], axis=1)
        values_t = jnp.concatenate([kv_t[j, :, BLK:] for j in slots], axis=1)
        dk = dv = None
        for p in range(ROWS // TALL):
            span = slice(p * TALL, (p + 1) * TALL)
            extra = terms[span, :]
            scores = jnp.dot(
                jnp.concatenate([pack[piece, span, :], extra], axis=1), keys_t, preferred_element_type=F32
            )
            prob = jnp.exp2(scores * (SCALE * LOG2E))
            if diagonal:
                query_at = lax.broadcasted_iota(jnp.int32, (TALL, n), 0) % BLK
                key_at = lax.broadcasted_iota(jnp.int32, (TALL, n), 1)
                prob = jnp.where((key_at <= query_at) | (key_at >= BLK), prob, 0.0)
            prob_grad = jnp.dot(
                jnp.concatenate([pack[piece, ROWS + p * TALL : ROWS + (p + 1) * TALL, :], extra], axis=1),
                values_t,
                preferred_element_type=F32,
            )
            dscore = (prob * prob_grad).astype(BF16)
            dv_part = jnp.dot(gradient_t[:, span], prob.astype(BF16), preferred_element_type=F32)
            dk_part = jnp.dot(query_t[:, span], dscore, preferred_element_type=F32)
            dv = dv_part if dv is None else dv + dv_part
            dk = dk_part if dk is None else dk + dk_part
            part = jnp.dot(dscore, keys, preferred_element_type=F32)
            if diagonal:
                dq_acc[span, :] = part
            else:
                dq_acc[span, :] += part
        for m, j in enumerate(slots):
            acc[j, 0:BLK, :] += dk[:, m * BLK : (m + 1) * BLK]
            acc[j, BLK:, :] += dv[:, m * BLK : (m + 1) * BLK]

    @pl.loop(0, PAIR)
    def _(piece):
        lane = lax.broadcasted_iota(jnp.int32, (BLK, 128), 1)
        columns = jnp.concatenate(
            [pack[piece, 2 * ROWS : 2 * ROWS + 32, :].astype(F32), jnp.zeros((BLK - 32, BLK), F32)], axis=0
        ).T
        for h in range(GROUP):
            cols = slice(h * BLK, (h + 1) * BLK)
            query_t[:, cols] = pack[piece, cols, :].T
            gradient_t[:, cols] = pack[piece, ROWS + h * BLK : ROWS + (h + 1) * BLK, :].T
            terms[cols, :] = jnp.where(lane % GROUP == h, columns, 0.0).astype(BF16)

        side = piece + first
        block = ring * SIDE + (own ^ side)
        above = lax.while_loop(lambda c: c[0] > 0, lambda c: (parents[0, c[0]], c[1] + 1), (block, 0))[1]
        odd = above % 2 == 1

        @pl.when(odd)
        def _():
            tile(piece, [side, slot_of(parents[0, block])], True)

        @pl.when(jnp.logical_not(odd))
        def _():
            tile(piece, [side], True)

        def ancestors(at):
            one = parents[0, at]
            two = parents[0, one]
            tile(piece, [slot_of(one), slot_of(two)], False)
            return two

        def quad(c):
            at, left = c
            one = parents[0, at]
            two = parents[0, one]
            three = parents[0, two]
            four = parents[0, three]
            tile(piece, [slot_of(one), slot_of(two), slot_of(three), slot_of(four)], False)
            return four, left - 4

        start = jnp.where(odd, parents[0, block], block)
        at, left = lax.while_loop(lambda c: c[1] >= 4, quad, (start, above - odd.astype(jnp.int32)))

        @pl.when(left > 0)
        def _():
            ancestors(at)

        dq[piece] = (dq_acc[...] * SCALE).astype(BF16)
        for k in range(PAIR):

            @pl.when(piece == k)
            def _(k=k):
                store_dq(k).start()

    stores = [store_dq(k) for k in range(PAIR)]
    if not last:
        stores.append(pltpu.make_async_copy(acc, sums_out, out_sem.at[PAIR]))
        stores[-1].start()
        for store in stores:
            store.wait()
        return
    for s in RING_ORDER + (0,):
        for k in range(SIDE):
            dk, dv = acc[s * SIDE + k, 0:BLK, :] * SCALE, acc[s * SIDE + k, BLK:, :]
            at = 2 * k * BLK
            if s == 0:
                stage_own[at : at + BLK, :] = dk.T
                stage_own[at + BLK : at + 2 * BLK, :] = dv.T
            else:
                stage[s - 1, at : at + BLK, :] = dk.astype(BF16).T
                stage[s - 1, at + BLK : at + 2 * BLK, :] = dv.astype(BF16).T
        source = stage_own if s == 0 else stage.at[s - 1]
        stores.append(pltpu.make_async_copy(source, grad_outs[s], out_sem.at[PAIR + s]))
        stores[-1].start()
    for store in stores:
        store.wait()


def attention_call(place, parents, kv, packs, first, *rest):
    sum_shape = (RING * SIDE, 2 * BLK, HEAD_SIZE)
    hbm = pl.BlockSpec(memory_space=pl.ANY)
    if first:
        out_shape = [shape(PAIR * ROWS + 4 * BLK), shape(ROWS, kind=F32)] + [shape(ROWS)] * (RING - 1)
    else:
        out_shape = [shape(PAIR * ROWS), jax.ShapeDtypeStruct(sum_shape, F32)]
    return pl.pallas_call(
        functools.partial(attention_kernel, first),
        out_shape=out_shape,
        in_specs=[smem()] * 2 + [hbm] * (RING + PAIR + len(rest)),
        out_specs=[hbm] * len(out_shape),
        scratch_shapes=[
            pltpu.VMEM(sum_shape, BF16),
            pltpu.VMEM((RING * SIDE, 2 * HEAD_SIZE, 2 * BLK), BF16),
            pltpu.VMEM((PAIR, PACK, HEAD_SIZE), BF16),
            pltpu.VMEM((HEAD_SIZE, ROWS), BF16),
            pltpu.VMEM((HEAD_SIZE, ROWS), BF16),
            pltpu.VMEM((ROWS, 128), BF16),
            pltpu.VMEM((ROWS, HEAD_SIZE), F32),
            pltpu.VMEM((PAIR, ROWS, HEAD_SIZE), BF16),
            pltpu.VMEM(sum_shape, F32),
            pltpu.VMEM((ROWS, HEAD_SIZE), F32),
            pltpu.VMEM((RING - 1, ROWS, HEAD_SIZE), BF16),
            pltpu.SemaphoreType.DMA((RING * SIDE,)),
            pltpu.SemaphoreType.DMA((PAIR + 1,)),
            pltpu.SemaphoreType.DMA((PAIR + RING,)),
        ],
        compiler_params=pltpu.CompilerParams(vmem_limit_bytes=24 * MIB),
        cost_estimate=pl.CostEstimate(flops=0, bytes_accessed=0, transcendentals=0),
    )(place, parents, *kv, *packs, *rest)


def total_kernel(grad_own, *refs):
    parts, (total, _, side, sem) = refs[: RING - 1], refs[RING + 2 :]
    value = grad_own[...]
    for part in parts:
        value = value + part[...].astype(F32)
    total[...] = value.astype(BF16)
    store = pltpu.make_async_copy(
        total.at[pl.ds(4 * BLK, 4 * BLK), :], side.at[pl.ds(2 * ROWS, 4 * BLK), :], sem
    )
    store.start()
    store.wait()


def total_call(grad_own, received, inputs, side, after):
    hbm = pl.BlockSpec(memory_space=pl.ANY)
    return pl.pallas_call(
        total_kernel,
        out_shape=[shape(ROWS), shape(*inputs.shape), shape(*side.shape)],
        in_specs=[vmem()] * RING + [hbm] * 3,
        out_specs=[vmem(), hbm, hbm],
        scratch_shapes=[pltpu.SemaphoreType.DMA],
        input_output_aliases={RING: 1, RING + 1: 2},
        compiler_params=pltpu.CompilerParams(vmem_limit_bytes=16 * MIB),
        cost_estimate=pl.CostEstimate(flops=0, bytes_accessed=0, transcendentals=0),
    )(grad_own, *received, inputs, side, after)


def relay_kernel(near, side, total, *rest):
    out = rest[-1]
    out[0:ROWS, :] = side[ROWS : 2 * ROWS, :]
    out[ROWS : ROWS + 2 * BLK, :] = total[2 * BLK : 4 * BLK, :]
    out[ROWS + 2 * BLK : ROWS + 4 * BLK, :] = side[2 * ROWS + 2 * BLK :, :]
    out[ROWS + 4 * BLK :, :] = near[ROWS:, :]


def join_inputs_kernel(*refs):
    pieces, out = refs[:RING], refs[-1]
    for s in range(RING):
        out[s * BLK : (s + 1) * BLK, :] = pieces[s][...]


def projection_kernel(*refs):
    grads = dict(zip((0,) + RING_ORDER, refs[:RING]))
    inputs = refs[RING : RING + SIDE]
    out, grad_t, weight_t, keys, values = refs[RING + SIDE :]
    for s in range(RING):
        for k in range(SIDE):
            at = 2 * k * BLK
            grad_t[k, 0:BLK, s * BLK : (s + 1) * BLK] = grads[s][at : at + BLK, :].T
            grad_t[k, BLK:, s * BLK : (s + 1) * BLK] = grads[s][at + BLK : at + 2 * BLK, :].T
    total = jnp.dot(grad_t[0], inputs[0][...], preferred_element_type=F32)
    for k in range(1, SIDE):
        total = total + jnp.dot(grad_t[k], inputs[k][...], preferred_element_type=F32)
    weight_t[...] = total
    for n in range(keys.shape[0] // BLK):
        rows = slice(n * BLK, (n + 1) * BLK)
        keys[rows, :] = weight_t[0:BLK, rows].T
        values[rows, :] = weight_t[BLK:, rows].T
    count, both, _ = out.shape
    for j in range(count):
        rows = slice(j * (both // 2), (j + 1) * (both // 2))
        out[j] = jnp.concatenate([keys[rows, :], values[rows, :]], axis=0).astype(BF16)


def weight_kernel(parts, out):
    share = out.shape[0]
    for g in range(KEY_VALUE_HEADS):
        total = parts[g].astype(F32)
        for d in range(1, TREES):
            total = total + parts[d * SIDE + g].astype(F32)
        out[:, g * HEAD_SIZE : (g + 1) * HEAD_SIZE] = total[0:share]
        col = (KEY_VALUE_HEADS + g) * HEAD_SIZE
        out[:, col : col + HEAD_SIZE] = total[share:]


def join_kernel(place, near, side, crossed, total, queries, keys, values):
    own = place[1]
    kv_at = ROWS + 4 * BLK
    for h in range(GROUP):
        rows = slice(h * BLK, (h + 1) * BLK)
        last = slice(kv_at + h * BLK, kv_at + (h + 1) * BLK)
        for k, piece in enumerate((near[rows, :], crossed[last, :], side[rows, :], crossed[rows, :])):
            col = pl.multiple_of((own ^ k) * (GROUP * HEAD_SIZE) + h * HEAD_SIZE, HEAD_SIZE)
            queries[:, pl.ds(col, HEAD_SIZE)] = piece
    for k, (ref, at) in enumerate(((total, 0), (crossed, ROWS), (side, 2 * ROWS), (crossed, ROWS + 2 * BLK))):
        col = pl.multiple_of((own ^ k) * HEAD_SIZE, HEAD_SIZE)
        keys[:, pl.ds(col, HEAD_SIZE)] = ref[at : at + BLK, :]
        values[:, pl.ds(col, HEAD_SIZE)] = ref[at + BLK : at + 2 * BLK, :]


def shape(rows, cols=HEAD_SIZE, kind=BF16):
    return jax.ShapeDtypeStruct((rows, cols), kind)


def local(
    queries,
    key_tensor,
    value_tensor,
    attention_output,
    output_gradient,
    logsumexp_rows,
    layer_input,
    parents,
    trees,
):
    width = layer_input.shape[2]
    quarter = width // RING
    share = width // (trees * RING * SIDE)
    at = lax.axis_index("ctx")
    ring, own = at // SIDE, at % SIDE
    place = jnp.stack([ring, own]).astype(jnp.int32)

    def to_side(x, k):
        return lax.ppermute(x, "ctx", side_perm(k))

    def to_ring(x, s):
        return lax.ppermute(x, "ctx", ring_perm(s % RING))

    with jax.named_scope("keys_values"):
        kv_split = call(split_kv_kernel, [shape(2 * BLK)] * SIDE, 1, 2, limit=56)(
            place, key_tensor[0], value_tensor[0]
        )
        kv_far = [to_side(kv_split[k], k) for k in (2, 3)]

    query_args = (queries[0], output_gradient[0], attention_output[0], logsumexp_rows[0], kv_split[1])
    with jax.named_scope("queries_near"):
        near_own = split_queries(place, *query_args, kv_split[2], 0)
        packs_near = [near_own[0], to_side(near_own[1], 1)]

    with jax.named_scope("keys_values_ring"):
        kv_own, token = call(stack_kernel, [shape(ROWS), shape(8, 128, F32)], 0, SIDE)(
            kv_split[0], packs_near[1], *kv_far
        )
        kv = {s: to_ring(kv_own, s) for s in RING_ORDER}
        kv = [kv_own] + [kv[s] for s in (1, 2, 3)]

    with jax.named_scope("queries_far"):
        far_own = split_queries(place, *query_args, token, 2)
        packs_far = [to_side(far_own[k - 2], k) for k in (2, 3)]

    with jax.named_scope("inputs_ring"):
        shares = call(
            share_inputs_kernel,
            [shape(BLK, quarter)] * RING,
            1,
            1,
            n_any=4,
            scratch=[pltpu.VMEM((RING, BLK, quarter), BF16)],
        )(place, layer_input[0], *kv[1:], packs_near[1])
        from_ring = {s: to_ring(shares[s], s) for s in RING_ORDER}
        from_ring = [shares[0]] + [from_ring[s] for s in (1, 2, 3)]

    with jax.named_scope("attention_near"):
        dq_near, sums = attention_call(place, parents, kv, packs_near, 0)

    with jax.named_scope("inputs_side"):
        input_own = call(join_inputs_kernel, [shape(RING * BLK, quarter)], 0, RING, n_any=3)(
            *from_ring, *packs_far, dq_near
        )[0]
        input_y = to_side(input_own, 2)
        input_core = to_side(input_own, 1)

    with jax.named_scope("attention_far"):
        outs = attention_call(place, parents, kv, packs_far, 2, sums, input_own)
        side_out, grad_own, grad_parts = outs[0], outs[1], outs[2:]

    with jax.named_scope("kv_gradients"):
        received = [to_ring(grad_parts[s - 1], -s) for s in RING_ORDER]
        grad_total, input_y, side_out = total_call(grad_own, received, input_y, side_out, input_core)
        input_last = to_side(input_y, 1)
        grads = [grad_total] + [to_ring(grad_total, s) for s in RING_ORDER]

    with jax.named_scope("projection"):
        partial = call(
            projection_kernel,
            [jax.ShapeDtypeStruct((trees * SIDE, 2 * share, HEAD_SIZE), BF16)],
            0,
            RING + SIDE,
            scratch=[
                pltpu.VMEM((SIDE, 2 * BLK, RING * BLK), BF16),
                pltpu.VMEM((2 * BLK, quarter), F32),
                pltpu.VMEM((quarter, HEAD_SIZE), F32),
                pltpu.VMEM((quarter, HEAD_SIZE), F32),
            ],
        )(*grads, input_own, input_core, input_y, input_last)[0]

    with jax.named_scope("own_gradients"):
        side = to_side(side_out, 2)
        crossed = to_side(
            call(relay_kernel, [shape(2 * ROWS + 4 * BLK)], 0, 3, n_any=3)(dq_near, side, grad_total, *grads[1:])[0], 1
        )
        grad_queries, grad_keys, grad_values = call(
            join_kernel,
            [shape(BLK, QUERY_HEADS * HEAD_SIZE)] + [shape(BLK, KEY_VALUE_HEADS * HEAD_SIZE)] * 2,
            1,
            4,
            moved=64 * MIB,
        )(place, dq_near, side, crossed, grad_total)

    with jax.named_scope("projection_sum"):
        groups = [
            [d * RING * SIDE + r * SIDE + g for d in range(trees) for g in range(SIDE)]
            for r in range(RING)
        ]
        swapped = lax.all_to_all(partial, ("dp", "ctx"), 0, 0, axis_index_groups=groups, tiled=True)
        grad_kv_weight = call(weight_kernel, [shape(share, 2 * KEY_VALUE_HEADS * HEAD_SIZE, F32)], 0, 1)(swapped)[0]

    return grad_queries[None], grad_keys[None], grad_values[None], grad_kv_weight


def solution(mesh):
    in_specs = (
        P("dp", "ctx", None),
        P("dp", "ctx", None),
        P("dp", "ctx", None),
        P("dp", "ctx", None),
        P("dp", "ctx", None),
        P("dp", None, "ctx"),
        P("dp", "ctx", None),
        P("dp", None),
    )
    out_specs = (
        P("dp", "ctx", None),
        P("dp", "ctx", None),
        P("dp", "ctx", None),
        P(("dp", "ctx"), None),
    )
    return jax.shard_map(
        functools.partial(local, trees=mesh.shape["dp"]),
        mesh=mesh,
        in_specs=in_specs,
        out_specs=out_specs,
        check_vma=False,
    )
```

```python
import functools

import jax
import jax.numpy as jnp
from jax import lax
from jax.experimental import pallas as pl
from jax.experimental.pallas import tpu as pltpu
from jax.sharding import PartitionSpec as P

QUERY_HEADS = 32
KEY_VALUE_HEADS = 4
HEAD_SIZE = 128
BLK = 128
GROUP = QUERY_HEADS // KEY_VALUE_HEADS
RING = 4
SIDE = 4
TREES = 8
PAIR = 2
TALL = 1024
ROWS = GROUP * BLK
PACK = 2 * ROWS + 32
SCALE = HEAD_SIZE ** (-0.5)
RING_ORDER = (2, 1, 3)
KV_ORDER = (0, 1, 3, 2)
LOG2E = 1.4426950408889634
LSE_SCALE = HEAD_SIZE**0.5
F32 = jnp.float32
BF16 = jnp.bfloat16
MIB = 1 << 20


def side_perm(k):
    return [(c, c ^ k) for c in range(RING * SIDE)]


def ring_perm(s):
    return [(c, ((c // SIDE + s) % RING) * SIDE + c % SIDE) for c in range(RING * SIDE)]


def smem():
    return pl.BlockSpec(memory_space=pltpu.SMEM)


def vmem():
    return pl.BlockSpec(memory_space=pltpu.VMEM)


def call(kernel, out_shape, n_smem, n_vmem, n_any=0, scratch=(), moved=0, limit=20):
    return pl.pallas_call(
        kernel,
        out_shape=out_shape,
        in_specs=[smem()] * n_smem + [vmem()] * n_vmem + [pl.BlockSpec(memory_space=pl.ANY)] * n_any,
        out_specs=[vmem()] * len(out_shape),
        scratch_shapes=list(scratch),
        compiler_params=pltpu.CompilerParams(vmem_limit_bytes=limit * MIB),
        cost_estimate=pl.CostEstimate(flops=0, bytes_accessed=moved, transcendentals=0),
    )


def split_queries_kernel(near, place, query_ref, gradient_ref, output_ref, lse_ref, *refs):
    if near:
        key_ref, value_ref, outs = refs[0], refs[1], refs[2:]
        kv_outs, outs = outs[-3:], outs[:-3]
    else:
        outs = refs[1:]
    outs, token = outs[:-1], outs[-1]
    token[...] = jnp.zeros_like(token)
    lane = lax.broadcasted_iota(jnp.int32, (BLK, 128), 1)
    columns = jnp.zeros((BLK, 128), F32)
    for h in range(GROUP):
        cols = slice(h * HEAD_SIZE, (h + 1) * HEAD_SIZE)
        prod = gradient_ref[:, cols].astype(F32) * output_ref[:, cols].astype(F32)
        columns = jnp.where(lane == h, jnp.sum(prod, axis=1, keepdims=True), columns)
    delta = columns.T[0:GROUP]
    lse = lse_ref[...] * LSE_SCALE

    def split(rows):
        high = rows.astype(BF16)
        low = (rows - high.astype(F32)).astype(BF16)
        return jnp.concatenate([high, low], axis=0)

    if near:

        @pl.when(pl.program_id(0) == 0)
        def _():
            for k, out in ((0, kv_outs[0]), (1, outs[1].at[pl.ds(PACK, 2 * BLK), :]), (2, kv_outs[1]), (3, kv_outs[2])):
                col = pl.multiple_of((place[1] ^ k) * HEAD_SIZE, HEAD_SIZE)
                out[0:BLK, :] = key_ref[:, pl.ds(col, HEAD_SIZE)]
                out[BLK:, :] = value_ref[:, pl.ds(col, HEAD_SIZE)]

    for k, out in enumerate(outs):

        @pl.when(pl.program_id(0) == k)
        def _(out=out):
            for h in range(GROUP):
                cols = slice(h * HEAD_SIZE, (h + 1) * HEAD_SIZE)
                out[h * BLK : (h + 1) * BLK, :] = query_ref[:, cols]
                out[ROWS + h * BLK : ROWS + (h + 1) * BLK, :] = gradient_ref[:, cols]
            out[2 * ROWS : 2 * ROWS + 16, :] = split(lse)
            out[2 * ROWS + 16 : 2 * ROWS + 32, :] = split(delta)


def split_queries(place, queries, gradient, output, lse, first, *rest):
    count = SIDE // 2
    near = first == 0
    kv_whole = pl.BlockSpec((BLK, KEY_VALUE_HEADS * HEAD_SIZE), lambda k, place: (0, 0))
    kv_piece = pl.BlockSpec((2 * BLK, HEAD_SIZE), lambda k, place: (0, 0))
    rows = PACK if first else PACK + 2 * BLK
    wide = pl.BlockSpec((BLK, GROUP * HEAD_SIZE), lambda k, place: (0, place[1] ^ (first + k)))
    return pl.pallas_call(
        functools.partial(split_queries_kernel, near),
        out_shape=[shape(rows)] * count + [shape(8, 128, F32)] + [shape(2 * BLK)] * (3 * near),
        grid_spec=pltpu.PrefetchScalarGridSpec(
            num_scalar_prefetch=1,
            grid=(count,),
            in_specs=[
                wide,
                wide,
                wide,
                pl.BlockSpec((GROUP, BLK), lambda k, place: (place[1] ^ (first + k), 0)),
            ]
            + ([kv_whole] * 2 if near else [pl.BlockSpec(memory_space=pl.ANY)]),
            out_specs=[pl.BlockSpec((rows, HEAD_SIZE), lambda k, place: (0, 0))] * count
            + [pl.BlockSpec((8, 128), lambda k, place: (0, 0))]
            + [kv_piece] * (3 * near),
        ),
        compiler_params=pltpu.CompilerParams(vmem_limit_bytes=56 * MIB),
        cost_estimate=pl.CostEstimate(flops=0, bytes_accessed=32 * MIB, transcendentals=0),
    )(place, queries, gradient, output, lse, *rest)


def stack_kernel(*refs):
    out = refs[SIDE]
    rows = refs[0].shape[0]
    for k in range(SIDE):
        out[k * rows : (k + 1) * rows, :] = refs[k][refs[k].shape[0] - rows :, :]


def share_inputs_kernel(place, inputs, *refs):
    outs, shares = refs[-1 - RING : -1], refs[-1]
    _, _, quarter = shares.shape
    piece = quarter // TREES
    for r in range(RING):
        shares[r] = jnp.concatenate(
            [inputs[:, (d * RING + r) * piece : (d * RING + r + 1) * piece] for d in range(TREES)], axis=1
        )
    for s, out in enumerate(outs):
        out[...] = shares[(place[0] + s) % RING]


def attention_kernel(first, place, parents, *refs):
    last = first > 0
    kv_in, packs, refs = refs[:RING], refs[RING : RING + PAIR], refs[RING + PAIR :]
    kv_in = [kv_in[KV_ORDER.index(s)] for s in range(RING)]
    if last:
        sums_in, dq_out, grad_outs, refs = refs[0], refs[2], refs[3 : 3 + RING], refs[3 + RING :]
    else:
        dq_out, sums_out, refs = refs[0], refs[1], refs[2:]
    kv, kv_t, pack, query_t, gradient_t, terms, dq_acc, dq, kv_sem, pack_sem, out_sem = refs[:11]
    if last:
        acc, stage_own, stage = refs[11:]
    else:
        acc = sums_out
    ring, own = place[0], place[1]

    loads = []
    for s in range(RING):
        for k in range(SIDE):
            slot = s * SIDE + k
            source = kv_in[s].at[pl.ds(2 * k * BLK, 2 * BLK), :]
            loads.append(pltpu.make_async_copy(source, kv.at[slot], kv_sem.at[slot]))
    pack_loads = [
        pltpu.make_async_copy(packs[k].at[pl.ds(0, PACK), :], pack.at[k], pack_sem.at[k]) for k in range(PAIR)
    ]
    for load in loads + pack_loads:
        load.start()
    acc[...] = sums_in[...] if last else jnp.zeros_like(acc)
    for load in loads:
        load.wait()

    row = lax.broadcasted_iota(jnp.int32, (BLK, BLK), 0)
    minus_lse = jnp.where(row < 16, -1.0, 0.0).astype(BF16)
    minus_delta = jnp.where((row >= 16) & (row < 32), -1.0, 0.0).astype(BF16)

    @pl.loop(0, RING * SIDE // 4)
    def _(quarter):
        for part in range(4):
            j = quarter * 4 + part
            kv_t[j, 0:BLK, 0:BLK] = kv[j, 0:BLK, :].T
            kv_t[j, 0:BLK, BLK:] = kv[j, BLK:, :].T
            kv_t[j, BLK:, 0:BLK] = minus_lse
            kv_t[j, BLK:, BLK:] = minus_delta

    for load in pack_loads:
        load.wait()

    def store_dq(k):
        return pltpu.make_async_copy(dq.at[k], dq_out.at[pl.ds(k * ROWS, ROWS), :], out_sem.at[k])

    def slot_of(at):
        return ((ring - at // SIDE) % RING) * SIDE + ((at % SIDE) ^ own)

    def tile(piece, slots, diagonal):
        n = len(slots) * BLK
        keys = jnp.concatenate([kv[j, 0:BLK, :] for j in slots], axis=0)
        keys_t = jnp.concatenate([kv_t[j, :, 0:BLK] for j in slots], axis=1)
        values_t = jnp.concatenate([kv_t[j, :, BLK:] for j in slots], axis=1)
        dk = dv = None
        for p in range(ROWS // TALL):
            span = slice(p * TALL, (p + 1) * TALL)
            extra = terms[span, :]
            scores = jnp.dot(
                jnp.concatenate([pack[piece, span, :], extra], axis=1), keys_t, preferred_element_type=F32
            )
            prob = jnp.exp2(scores * (SCALE * LOG2E))
            if diagonal:
                query_at = lax.broadcasted_iota(jnp.int32, (TALL, n), 0) % BLK
                key_at = lax.broadcasted_iota(jnp.int32, (TALL, n), 1)
                prob = jnp.where((key_at <= query_at) | (key_at >= BLK), prob, 0.0)
            prob_grad = jnp.dot(
                jnp.concatenate([pack[piece, ROWS + p * TALL : ROWS + (p + 1) * TALL, :], extra], axis=1),
                values_t,
                preferred_element_type=F32,
            )
            dscore = (prob * prob_grad).astype(BF16)
            dv_part = jnp.dot(gradient_t[:, span], prob.astype(BF16), preferred_element_type=F32)
            dk_part = jnp.dot(query_t[:, span], dscore, preferred_element_type=F32)
            dv = dv_part if dv is None else dv + dv_part
            dk = dk_part if dk is None else dk + dk_part
            part = jnp.dot(dscore, keys, preferred_element_type=F32)
            if diagonal:
                dq_acc[span, :] = part
            else:
                dq_acc[span, :] += part
        for m, j in enumerate(slots):
            acc[j, 0:BLK, :] += dk[:, m * BLK : (m + 1) * BLK]
            acc[j, BLK:, :] += dv[:, m * BLK : (m + 1) * BLK]

    @pl.loop(0, PAIR)
    def _(piece):
        lane = lax.broadcasted_iota(jnp.int32, (BLK, 128), 1)
        columns = jnp.concatenate(
            [pack[piece, 2 * ROWS : 2 * ROWS + 32, :].astype(F32), jnp.zeros((BLK - 32, BLK), F32)], axis=0
        ).T
        for h in range(GROUP):
            cols = slice(h * BLK, (h + 1) * BLK)
            query_t[:, cols] = pack[piece, cols, :].T
            gradient_t[:, cols] = pack[piece, ROWS + h * BLK : ROWS + (h + 1) * BLK, :].T
            terms[cols, :] = jnp.where(lane % GROUP == h, columns, 0.0).astype(BF16)

        side = piece + first
        block = ring * SIDE + (own ^ side)
        above = lax.while_loop(lambda c: c[0] > 0, lambda c: (parents[0, c[0]], c[1] + 1), (block, 0))[1]
        odd = above % 2 == 1

        @pl.when(odd)
        def _():
            tile(piece, [side, slot_of(parents[0, block])], True)

        @pl.when(jnp.logical_not(odd))
        def _():
            tile(piece, [side], True)

        def ancestors(at):
            one = parents[0, at]
            two = parents[0, one]
            tile(piece, [slot_of(one), slot_of(two)], False)
            return two

        def quad(c):
            at, left = c
            one = parents[0, at]
            two = parents[0, one]
            three = parents[0, two]
            four = parents[0, three]
            tile(piece, [slot_of(one), slot_of(two), slot_of(three), slot_of(four)], False)
            return four, left - 4

        start = jnp.where(odd, parents[0, block], block)
        at, left = lax.while_loop(lambda c: c[1] >= 4, quad, (start, above - odd.astype(jnp.int32)))

        @pl.when(left > 0)
        def _():
            ancestors(at)

        dq[piece] = (dq_acc[...] * SCALE).astype(BF16)
        for k in range(PAIR):

            @pl.when(piece == k)
            def _(k=k):
                store_dq(k).start()

    stores = [store_dq(k) for k in range(PAIR)]
    if not last:
        for store in stores:
            store.wait()
        return
    for s in RING_ORDER + (0,):
        for k in range(SIDE):
            dk, dv = acc[s * SIDE + k, 0:BLK, :] * SCALE, acc[s * SIDE + k, BLK:, :]
            at = 2 * k * BLK
            if s == 0:
                stage_own[at : at + BLK, :] = dk.T
                stage_own[at + BLK : at + 2 * BLK, :] = dv.T
            else:
                stage[s - 1, at : at + BLK, :] = dk.astype(BF16).T
                stage[s - 1, at + BLK : at + 2 * BLK, :] = dv.astype(BF16).T
        source = stage_own if s == 0 else stage.at[s - 1]
        stores.append(pltpu.make_async_copy(source, grad_outs[s], out_sem.at[PAIR + s]))
        stores[-1].start()
    for store in stores:
        store.wait()


def attention_call(place, parents, kv, packs, first, *rest):
    sum_shape = (RING * SIDE, 2 * BLK, HEAD_SIZE)
    hbm = pl.BlockSpec(memory_space=pl.ANY)
    last_scratch = []
    if first:
        last_scratch = [
            pltpu.VMEM(sum_shape, F32),
            pltpu.VMEM((ROWS, HEAD_SIZE), F32),
            pltpu.VMEM((RING - 1, ROWS, HEAD_SIZE), BF16),
        ]
        out_shape = [shape(PAIR * ROWS + 4 * BLK), shape(ROWS, kind=F32)] + [shape(ROWS)] * (RING - 1)
    else:
        out_shape = [shape(PAIR * ROWS), jax.ShapeDtypeStruct(sum_shape, F32)]
    return pl.pallas_call(
        functools.partial(attention_kernel, first),
        out_shape=out_shape,
        in_specs=[smem()] * 2 + [hbm] * (RING + PAIR) + ([vmem(), hbm] if first else []),
        out_specs=[hbm] * len(out_shape) if first else [hbm, vmem()],
        scratch_shapes=[
            pltpu.VMEM(sum_shape, BF16),
            pltpu.VMEM((RING * SIDE, 2 * HEAD_SIZE, 2 * BLK), BF16),
            pltpu.VMEM((PAIR, PACK, HEAD_SIZE), BF16),
            pltpu.VMEM((HEAD_SIZE, ROWS), BF16),
            pltpu.VMEM((HEAD_SIZE, ROWS), BF16),
            pltpu.VMEM((ROWS, 128), BF16),
            pltpu.VMEM((ROWS, HEAD_SIZE), F32),
            pltpu.VMEM((PAIR, ROWS, HEAD_SIZE), BF16),
            pltpu.SemaphoreType.DMA((RING * SIDE,)),
            pltpu.SemaphoreType.DMA((PAIR,)),
            pltpu.SemaphoreType.DMA((PAIR + RING,)),
        ]
        + last_scratch,
        compiler_params=pltpu.CompilerParams(vmem_limit_bytes=24 * MIB),
        cost_estimate=pl.CostEstimate(flops=0, bytes_accessed=0, transcendentals=0),
    )(place, parents, *[kv[s] for s in KV_ORDER], *packs, *rest)


def total_kernel(grad_own, *refs):
    parts, (total, _, side, sem) = refs[: RING - 1], refs[RING + 2 :]
    value = grad_own[...]
    for part in parts:
        value = value + part[...].astype(F32)
    total[...] = value.astype(BF16)
    store = pltpu.make_async_copy(
        total.at[pl.ds(4 * BLK, 4 * BLK), :], side.at[pl.ds(2 * ROWS, 4 * BLK), :], sem
    )
    store.start()
    store.wait()


def total_call(grad_own, received, inputs, side, after):
    hbm = pl.BlockSpec(memory_space=pl.ANY)
    return pl.pallas_call(
        total_kernel,
        out_shape=[shape(ROWS), shape(*inputs.shape), shape(*side.shape)],
        in_specs=[vmem()] * RING + [hbm] * 3,
        out_specs=[vmem(), hbm, hbm],
        scratch_shapes=[pltpu.SemaphoreType.DMA],
        input_output_aliases={RING: 1, RING + 1: 2},
        compiler_params=pltpu.CompilerParams(vmem_limit_bytes=16 * MIB),
        cost_estimate=pl.CostEstimate(flops=0, bytes_accessed=0, transcendentals=0),
    )(grad_own, *received, inputs, side, after)


def relay_kernel(near, side, total, *rest):
    out = rest[-1]
    out[0:ROWS, :] = side[ROWS : 2 * ROWS, :]
    out[ROWS : ROWS + 2 * BLK, :] = total[2 * BLK : 4 * BLK, :]
    out[ROWS + 2 * BLK : ROWS + 4 * BLK, :] = side[2 * ROWS + 2 * BLK :, :]
    out[ROWS + 4 * BLK :, :] = near[ROWS:, :]


def join_inputs_kernel(*refs):
    pieces, out = refs[:RING], refs[-1]
    for s, piece in zip((0,) + RING_ORDER, pieces):
        out[s * BLK : (s + 1) * BLK, :] = piece[...]


def projection_kernel(*refs):
    grads = dict(zip((0,) + RING_ORDER, refs[:RING]))
    inputs = refs[RING : RING + SIDE]
    out, grad_t, weight_t, keys, values = refs[RING + SIDE :]
    for s in range(RING):
        for k in range(SIDE):
            at = 2 * k * BLK
            grad_t[k, 0:BLK, s * BLK : (s + 1) * BLK] = grads[s][at : at + BLK, :].T
            grad_t[k, BLK:, s * BLK : (s + 1) * BLK] = grads[s][at + BLK : at + 2 * BLK, :].T
    total = jnp.dot(grad_t[0], inputs[0][...], preferred_element_type=F32)
    for k in range(1, SIDE):
        total = total + jnp.dot(grad_t[k], inputs[k][...], preferred_element_type=F32)
    weight_t[...] = total
    for n in range(keys.shape[0] // BLK):
        rows = slice(n * BLK, (n + 1) * BLK)
        keys[rows, :] = weight_t[0:BLK, rows].T
        values[rows, :] = weight_t[BLK:, rows].T
    count, both, _ = out.shape
    for j in range(count):
        rows = slice(j * (both // 2), (j + 1) * (both // 2))
        out[j] = jnp.concatenate([keys[rows, :], values[rows, :]], axis=0).astype(BF16)


def weight_kernel(parts, out):
    share = out.shape[0]
    for g in range(KEY_VALUE_HEADS):
        total = parts[g].astype(F32)
        for d in range(1, TREES):
            total = total + parts[d * SIDE + g].astype(F32)
        out[:, g * HEAD_SIZE : (g + 1) * HEAD_SIZE] = total[0:share]
        col = (KEY_VALUE_HEADS + g) * HEAD_SIZE
        out[:, col : col + HEAD_SIZE] = total[share:]


def join_kernel(place, near, side, crossed, total, queries, keys, values):
    own = place[1]
    kv_at = ROWS + 4 * BLK
    for h in range(GROUP):
        rows = slice(h * BLK, (h + 1) * BLK)
        last = slice(kv_at + h * BLK, kv_at + (h + 1) * BLK)
        for k, piece in enumerate((near[rows, :], crossed[last, :], side[rows, :], crossed[rows, :])):
            col = pl.multiple_of((own ^ k) * (GROUP * HEAD_SIZE) + h * HEAD_SIZE, HEAD_SIZE)
            queries[:, pl.ds(col, HEAD_SIZE)] = piece
    for k, (ref, at) in enumerate(((total, 0), (crossed, ROWS), (side, 2 * ROWS), (crossed, ROWS + 2 * BLK))):
        col = pl.multiple_of((own ^ k) * HEAD_SIZE, HEAD_SIZE)
        keys[:, pl.ds(col, HEAD_SIZE)] = ref[at : at + BLK, :]
        values[:, pl.ds(col, HEAD_SIZE)] = ref[at + BLK : at + 2 * BLK, :]


def shape(rows, cols=HEAD_SIZE, kind=BF16):
    return jax.ShapeDtypeStruct((rows, cols), kind)


def local(
    queries,
    key_tensor,
    value_tensor,
    attention_output,
    output_gradient,
    logsumexp_rows,
    layer_input,
    parents,
    trees,
):
    width = layer_input.shape[2]
    quarter = width // RING
    share = width // (trees * RING * SIDE)
    at = lax.axis_index("ctx")
    ring, own = at // SIDE, at % SIDE
    place = jnp.stack([ring, own]).astype(jnp.int32)

    def to_side(x, k):
        return lax.ppermute(x, "ctx", side_perm(k))

    def to_ring(x, s):
        return lax.ppermute(x, "ctx", ring_perm(s % RING))

    query_args = (queries[0], output_gradient[0], attention_output[0], logsumexp_rows[0])
    with jax.named_scope("near"):
        near_own = split_queries(place, *query_args, 0, key_tensor[0], value_tensor[0])
        packs_near = [near_own[0], to_side(near_own[1], 1)]
        kv_first = near_own[3]
        kv_far = [to_side(near_own[2 + k], k) for k in (2, 3)]

    with jax.named_scope("keys_values_ring"):
        kv_own, token = pl.pallas_call(
            stack_kernel,
            out_shape=[shape(ROWS), shape(8, 128, F32)],
            in_specs=[vmem()] * SIDE,
            out_specs=[vmem(), pl.BlockSpec(memory_space=pl.ANY)],
            compiler_params=pltpu.CompilerParams(vmem_limit_bytes=20 * MIB),
            cost_estimate=pl.CostEstimate(flops=0, bytes_accessed=0, transcendentals=0),
        )(kv_first, packs_near[1], *kv_far)
        kv = {s: to_ring(kv_own, s) for s in RING_ORDER}
        kv = [kv_own] + [kv[s] for s in (1, 2, 3)]

    with jax.named_scope("queries_far"):
        far_own = split_queries(place, *query_args, 2, token)
        packs_far = [to_side(far_own[k - 2], k) for k in (2, 3)]

    with jax.named_scope("inputs_ring"):
        shares = call(
            share_inputs_kernel,
            [shape(BLK, quarter)] * RING,
            1,
            1,
            n_any=4,
            scratch=[pltpu.VMEM((RING, BLK, quarter), BF16)],
        )(place, layer_input[0], kv[1], kv[3], kv[2], packs_near[1])
        from_ring = [shares[0]] + [to_ring(shares[s], s) for s in RING_ORDER]

    with jax.named_scope("attention_near"):
        dq_near, sums = attention_call(place, parents, kv, packs_near, 0)

    with jax.named_scope("inputs_side"):
        input_own = call(join_inputs_kernel, [shape(RING * BLK, quarter)], 0, RING, n_any=3)(
            *from_ring, *packs_far, dq_near
        )[0]
        input_y = to_side(input_own, 2)
        input_core = to_side(input_own, 1)

    with jax.named_scope("attention_far"):
        outs = attention_call(place, parents, kv, packs_far, 2, sums, input_own)
        side_out, grad_own, grad_parts = outs[0], outs[1], outs[2:]

    with jax.named_scope("kv_gradients"):
        received = [to_ring(grad_parts[s - 1], -s) for s in RING_ORDER]
        grad_total, input_y, side_out = total_call(grad_own, received, input_y, side_out, input_core)
        input_last = to_side(input_y, 1)
        grads = [grad_total] + [to_ring(grad_total, s) for s in RING_ORDER]

    with jax.named_scope("projection"):
        partial = call(
            projection_kernel,
            [jax.ShapeDtypeStruct((trees * SIDE, 2 * share, HEAD_SIZE), BF16)],
            0,
            RING + SIDE,
            scratch=[
                pltpu.VMEM((SIDE, 2 * BLK, RING * BLK), BF16),
                pltpu.VMEM((2 * BLK, quarter), F32),
                pltpu.VMEM((quarter, HEAD_SIZE), F32),
                pltpu.VMEM((quarter, HEAD_SIZE), F32),
            ],
        )(*grads, input_own, input_core, input_y, input_last)[0]

    with jax.named_scope("own_gradients"):
        side = to_side(side_out, 2)
        crossed = to_side(
            call(relay_kernel, [shape(2 * ROWS + 4 * BLK)], 0, 3, n_any=3)(dq_near, side, grad_total, *grads[:0:-1])[0], 1
        )
        grad_queries, grad_keys, grad_values = call(
            join_kernel,
            [shape(BLK, QUERY_HEADS * HEAD_SIZE)] + [shape(BLK, KEY_VALUE_HEADS * HEAD_SIZE)] * 2,
            1,
            4,
            moved=64 * MIB,
        )(place, dq_near, side, crossed, grad_total)

    with jax.named_scope("projection_sum"):
        groups = [
            [d * RING * SIDE + r * SIDE + g for d in range(trees) for g in range(SIDE)]
            for r in range(RING)
        ]
        swapped = lax.all_to_all(partial, ("dp", "ctx"), 0, 0, axis_index_groups=groups, tiled=True)
        grad_kv_weight = call(weight_kernel, [shape(share, 2 * KEY_VALUE_HEADS * HEAD_SIZE, F32)], 0, 1)(swapped)[0]

    return grad_queries[None], grad_keys[None], grad_values[None], grad_kv_weight


def solution(mesh):
    in_specs = (
        P("dp", "ctx", None),
        P("dp", "ctx", None),
        P("dp", "ctx", None),
        P("dp", "ctx", None),
        P("dp", "ctx", None),
        P("dp", None, "ctx"),
        P("dp", "ctx", None),
        P("dp", None),
    )
    out_specs = (
        P("dp", "ctx", None),
        P("dp", "ctx", None),
        P("dp", "ctx", None),
        P(("dp", "ctx"), None),
    )
    return jax.shard_map(
        functools.partial(local, trees=mesh.shape["dp"]),
        mesh=mesh,
        in_specs=in_specs,
        out_specs=out_specs,
        check_vma=False,
    )
```

```python
import functools

import jax
import jax.numpy as jnp
from jax import lax
from jax.experimental import pallas as pl
from jax.experimental.pallas import tpu as pltpu
from jax.sharding import PartitionSpec as P

QUERY_HEADS = 32
KEY_VALUE_HEADS = 4
HEAD_SIZE = 128
BLK = 128
GROUP = QUERY_HEADS // KEY_VALUE_HEADS
RING = 4
SIDE = 4
TREES = 8
PAIR = 2
TALL = 1024
ROWS = GROUP * BLK
PACK = 2 * ROWS + 32
SCALE = HEAD_SIZE ** (-0.5)
RING_ORDER = (2, 1, 3)
KV_ORDER = (0, 1, 3, 2)
LOG2E = 1.4426950408889634
LSE_SCALE = HEAD_SIZE**0.5
F32 = jnp.float32
BF16 = jnp.bfloat16
MIB = 1 << 20


def side_perm(k):
    return [(c, c ^ k) for c in range(RING * SIDE)]


def ring_perm(s):
    return [(c, ((c // SIDE + s) % RING) * SIDE + c % SIDE) for c in range(RING * SIDE)]


def smem():
    return pl.BlockSpec(memory_space=pltpu.SMEM)


def vmem():
    return pl.BlockSpec(memory_space=pltpu.VMEM)


def call(kernel, out_shape, n_smem, n_vmem, n_any=0, scratch=(), moved=0, limit=20):
    return pl.pallas_call(
        kernel,
        out_shape=out_shape,
        in_specs=[smem()] * n_smem + [vmem()] * n_vmem + [pl.BlockSpec(memory_space=pl.ANY)] * n_any,
        out_specs=[vmem()] * len(out_shape),
        scratch_shapes=list(scratch),
        compiler_params=pltpu.CompilerParams(vmem_limit_bytes=limit * MIB),
        cost_estimate=pl.CostEstimate(flops=0, bytes_accessed=moved, transcendentals=0),
    )


def split_queries_kernel(near, place, query_ref, gradient_ref, output_ref, lse_ref, *refs):
    if near:
        key_ref, value_ref, outs = refs[0], refs[1], refs[2:]
        kv_outs, outs = outs[-3:], outs[:-3]
    else:
        outs = refs[1:]
    outs, token = outs[:-1], outs[-1]
    token[...] = jnp.zeros_like(token)
    lane = lax.broadcasted_iota(jnp.int32, (BLK, 128), 1)
    columns = jnp.zeros((BLK, 128), F32)
    for h in range(GROUP):
        cols = slice(h * HEAD_SIZE, (h + 1) * HEAD_SIZE)
        prod = gradient_ref[:, cols].astype(F32) * output_ref[:, cols].astype(F32)
        columns = jnp.where(lane == h, jnp.sum(prod, axis=1, keepdims=True), columns)
    delta = columns.T[0:GROUP]
    lse = lse_ref[...] * LSE_SCALE

    def split(rows):
        high = rows.astype(BF16)
        low = (rows - high.astype(F32)).astype(BF16)
        return jnp.concatenate([high, low], axis=0)

    if near:

        @pl.when(pl.program_id(0) == 0)
        def _():
            for k, out in ((0, kv_outs[0]), (1, outs[1].at[pl.ds(PACK, 2 * BLK), :]), (2, kv_outs[1]), (3, kv_outs[2])):
                col = pl.multiple_of((place[1] ^ k) * HEAD_SIZE, HEAD_SIZE)
                out[0:BLK, :] = key_ref[:, pl.ds(col, HEAD_SIZE)]
                out[BLK:, :] = value_ref[:, pl.ds(col, HEAD_SIZE)]

    for k, out in enumerate(outs):

        @pl.when(pl.program_id(0) == k)
        def _(out=out):
            for h in range(GROUP):
                cols = slice(h * HEAD_SIZE, (h + 1) * HEAD_SIZE)
                out[h * BLK : (h + 1) * BLK, :] = query_ref[:, cols]
                out[ROWS + h * BLK : ROWS + (h + 1) * BLK, :] = gradient_ref[:, cols]
            out[2 * ROWS : 2 * ROWS + 16, :] = split(lse)
            out[2 * ROWS + 16 : 2 * ROWS + 32, :] = split(delta)


def split_queries(place, queries, gradient, output, lse, first, *rest):
    count = SIDE // 2
    near = first == 0
    kv_whole = pl.BlockSpec((BLK, KEY_VALUE_HEADS * HEAD_SIZE), lambda k, place: (0, 0))
    kv_piece = pl.BlockSpec((2 * BLK, HEAD_SIZE), lambda k, place: (0, 0))
    rows = PACK if first else PACK + 2 * BLK
    wide = pl.BlockSpec((BLK, GROUP * HEAD_SIZE), lambda k, place: (0, place[1] ^ (first + k)))
    return pl.pallas_call(
        functools.partial(split_queries_kernel, near),
        out_shape=[shape(rows)] * count + [shape(8, 128, F32)] + [shape(2 * BLK)] * (3 * near),
        grid_spec=pltpu.PrefetchScalarGridSpec(
            num_scalar_prefetch=1,
            grid=(count,),
            in_specs=[
                wide,
                wide,
                wide,
                pl.BlockSpec((GROUP, BLK), lambda k, place: (place[1] ^ (first + k), 0)),
            ]
            + ([kv_whole] * 2 if near else [pl.BlockSpec(memory_space=pl.ANY)]),
            out_specs=[pl.BlockSpec((rows, HEAD_SIZE), lambda k, place: (0, 0))] * count
            + [pl.BlockSpec((8, 128), lambda k, place: (0, 0))]
            + [kv_piece] * (3 * near),
        ),
        compiler_params=pltpu.CompilerParams(vmem_limit_bytes=56 * MIB),
        cost_estimate=pl.CostEstimate(flops=0, bytes_accessed=32 * MIB, transcendentals=0),
    )(place, queries, gradient, output, lse, *rest)


def stack_kernel(*refs):
    out = refs[SIDE]
    rows = refs[0].shape[0]
    for k in range(SIDE):
        out[k * rows : (k + 1) * rows, :] = refs[k][refs[k].shape[0] - rows :, :]


def share_inputs_kernel(place, inputs, *refs):
    outs, shares = refs[-1 - RING : -1], refs[-1]
    _, _, quarter = shares.shape
    piece = quarter // TREES
    for r in range(RING):
        shares[r] = jnp.concatenate(
            [inputs[:, (d * RING + r) * piece : (d * RING + r + 1) * piece] for d in range(TREES)], axis=1
        )
    for s, out in enumerate(outs):
        out[...] = shares[(place[0] + s) % RING]


def attention_kernel(first, place, parents, *refs):
    last = first > 0
    kv_in, packs, refs = refs[:RING], refs[RING : RING + PAIR], refs[RING + PAIR :]
    kv_in = [kv_in[KV_ORDER.index(s)] for s in range(RING)]
    if last:
        sums_in, dq_out, grad_outs, refs = refs[0], refs[2], refs[3 : 3 + RING], refs[3 + RING :]
    else:
        dq_out, sums_out, refs = refs[0], refs[1], refs[2:]
    kv, kv_t, pack, query_t, gradient_t, terms, dq_acc, dq, kv_sem, pack_sem, out_sem = refs[:11]
    if last:
        acc, stage_own, stage = refs[11:]
    else:
        acc = sums_out
    ring, own = place[0], place[1]

    loads = []
    for s in range(RING):
        for k in range(SIDE):
            slot = s * SIDE + k
            source = kv_in[s].at[pl.ds(2 * k * BLK, 2 * BLK), :]
            loads.append(pltpu.make_async_copy(source, kv.at[slot], kv_sem.at[slot]))
    pack_loads = [
        pltpu.make_async_copy(packs[k].at[pl.ds(0, PACK), :], pack.at[k], pack_sem.at[k]) for k in range(PAIR)
    ]
    for load in loads + pack_loads:
        load.start()
    acc[...] = sums_in[...] if last else jnp.zeros_like(acc)
    for load in loads:
        load.wait()

    row = lax.broadcasted_iota(jnp.int32, (BLK, BLK), 0)
    minus_lse = jnp.where(row < 16, -1.0, 0.0).astype(BF16)
    minus_delta = jnp.where((row >= 16) & (row < 32), -1.0, 0.0).astype(BF16)

    @pl.loop(0, RING * SIDE // 4)
    def _(quarter):
        for part in range(4):
            j = quarter * 4 + part
            kv_t[j, 0:BLK, 0:BLK] = kv[j, 0:BLK, :].T
            kv_t[j, 0:BLK, BLK:] = kv[j, BLK:, :].T
            kv_t[j, BLK:, 0:BLK] = minus_lse
            kv_t[j, BLK:, BLK:] = minus_delta

    for load in pack_loads:
        load.wait()

    def store_dq(k):
        return pltpu.make_async_copy(dq.at[k], dq_out.at[pl.ds(k * ROWS, ROWS), :], out_sem.at[k])

    def slot_of(at):
        return ((ring - at // SIDE) % RING) * SIDE + ((at % SIDE) ^ own)

    def tile(piece, slots, diagonal):
        n = len(slots) * BLK
        keys = jnp.concatenate([kv[j, 0:BLK, :] for j in slots], axis=0)
        keys_t = jnp.concatenate([kv_t[j, :, 0:BLK] for j in slots], axis=1)
        values_t = jnp.concatenate([kv_t[j, :, BLK:] for j in slots], axis=1)
        dk = dv = None
        for p in range(ROWS // TALL):
            span = slice(p * TALL, (p + 1) * TALL)
            extra = terms[span, :]
            scores = jnp.dot(
                jnp.concatenate([pack[piece, span, :], extra], axis=1), keys_t, preferred_element_type=F32
            )
            prob = jnp.exp2(scores * (SCALE * LOG2E))
            if diagonal:
                query_at = lax.broadcasted_iota(jnp.int32, (TALL, n), 0) % BLK
                key_at = lax.broadcasted_iota(jnp.int32, (TALL, n), 1)
                prob = jnp.where((key_at <= query_at) | (key_at >= BLK), prob, 0.0)
            prob_grad = jnp.dot(
                jnp.concatenate([pack[piece, ROWS + p * TALL : ROWS + (p + 1) * TALL, :], extra], axis=1),
                values_t,
                preferred_element_type=F32,
            )
            dscore = (prob * prob_grad).astype(BF16)
            dv_part = jnp.dot(gradient_t[:, span], prob.astype(BF16), preferred_element_type=F32)
            dk_part = jnp.dot(query_t[:, span], dscore, preferred_element_type=F32)
            dv = dv_part if dv is None else dv + dv_part
            dk = dk_part if dk is None else dk + dk_part
            part = jnp.dot(dscore, keys, preferred_element_type=F32)
            if diagonal:
                dq_acc[span, :] = part
            else:
                dq_acc[span, :] += part
        for m, j in enumerate(slots):
            acc[j, 0:BLK, :] += dk[:, m * BLK : (m + 1) * BLK]
            acc[j, BLK:, :] += dv[:, m * BLK : (m + 1) * BLK]

    @pl.loop(0, PAIR)
    def _(piece):
        lane = lax.broadcasted_iota(jnp.int32, (BLK, 128), 1)
        columns = jnp.concatenate(
            [pack[piece, 2 * ROWS : 2 * ROWS + 32, :].astype(F32), jnp.zeros((BLK - 32, BLK), F32)], axis=0
        ).T
        for h in range(GROUP):
            cols = slice(h * BLK, (h + 1) * BLK)
            query_t[:, cols] = pack[piece, cols, :].T
            gradient_t[:, cols] = pack[piece, ROWS + h * BLK : ROWS + (h + 1) * BLK, :].T
            terms[cols, :] = jnp.where(lane % GROUP == h, columns, 0.0).astype(BF16)

        side = piece + first
        block = ring * SIDE + (own ^ side)
        above = lax.while_loop(lambda c: c[0] > 0, lambda c: (parents[0, c[0]], c[1] + 1), (block, 0))[1]
        odd = above % 2 == 1

        @pl.when(odd)
        def _():
            tile(piece, [side, slot_of(parents[0, block])], True)

        @pl.when(jnp.logical_not(odd))
        def _():
            tile(piece, [side], True)

        def ancestors(at):
            one = parents[0, at]
            two = parents[0, one]
            tile(piece, [slot_of(one), slot_of(two)], False)
            return two

        def quad(c):
            at, left = c
            one = parents[0, at]
            two = parents[0, one]
            three = parents[0, two]
            four = parents[0, three]
            tile(piece, [slot_of(one), slot_of(two), slot_of(three), slot_of(four)], False)
            return four, left - 4

        start = jnp.where(odd, parents[0, block], block)
        at, left = lax.while_loop(lambda c: c[1] >= 4, quad, (start, above - odd.astype(jnp.int32)))

        @pl.when(left > 0)
        def _():
            ancestors(at)

        dq[piece] = (dq_acc[...] * SCALE).astype(BF16)
        for k in range(PAIR):

            @pl.when(piece == k)
            def _(k=k):
                store_dq(k).start()

    stores = [store_dq(k) for k in range(PAIR)]
    if not last:
        for store in stores:
            store.wait()
        return
    for s in RING_ORDER + (0,):
        for k in range(SIDE):
            dk, dv = acc[s * SIDE + k, 0:BLK, :] * SCALE, acc[s * SIDE + k, BLK:, :]
            at = 2 * k * BLK
            if s == 0:
                stage_own[at : at + BLK, :] = dk.T
                stage_own[at + BLK : at + 2 * BLK, :] = dv.T
            else:
                stage[s - 1, at : at + BLK, :] = dk.astype(BF16).T
                stage[s - 1, at + BLK : at + 2 * BLK, :] = dv.astype(BF16).T
        source = stage_own if s == 0 else stage.at[s - 1]
        stores.append(pltpu.make_async_copy(source, grad_outs[s], out_sem.at[PAIR + s]))
        stores[-1].start()
    for store in stores:
        store.wait()


def attention_call(place, parents, kv, packs, first, *rest):
    sum_shape = (RING * SIDE, 2 * BLK, HEAD_SIZE)
    hbm = pl.BlockSpec(memory_space=pl.ANY)
    last_scratch = []
    if first:
        last_scratch = [
            pltpu.VMEM(sum_shape, F32),
            pltpu.VMEM((ROWS, HEAD_SIZE), F32),
            pltpu.VMEM((RING - 1, ROWS, HEAD_SIZE), BF16),
        ]
        out_shape = [shape(PAIR * ROWS + 4 * BLK), shape(ROWS, kind=F32)] + [shape(ROWS)] * (RING - 1)
    else:
        out_shape = [shape(PAIR * ROWS), jax.ShapeDtypeStruct(sum_shape, F32)]
    return pl.pallas_call(
        functools.partial(attention_kernel, first),
        out_shape=out_shape,
        in_specs=[smem()] * 2 + [hbm] * (RING + PAIR) + ([vmem(), hbm] if first else []),
        out_specs=[hbm] * len(out_shape) if first else [hbm, vmem()],
        scratch_shapes=[
            pltpu.VMEM(sum_shape, BF16),
            pltpu.VMEM((RING * SIDE, 2 * HEAD_SIZE, 2 * BLK), BF16),
            pltpu.VMEM((PAIR, PACK, HEAD_SIZE), BF16),
            pltpu.VMEM((HEAD_SIZE, ROWS), BF16),
            pltpu.VMEM((HEAD_SIZE, ROWS), BF16),
            pltpu.VMEM((ROWS, 128), BF16),
            pltpu.VMEM((ROWS, HEAD_SIZE), F32),
            pltpu.VMEM((PAIR, ROWS, HEAD_SIZE), BF16),
            pltpu.SemaphoreType.DMA((RING * SIDE,)),
            pltpu.SemaphoreType.DMA((PAIR,)),
            pltpu.SemaphoreType.DMA((PAIR + RING,)),
        ]
        + last_scratch,
        compiler_params=pltpu.CompilerParams(vmem_limit_bytes=24 * MIB),
        cost_estimate=pl.CostEstimate(flops=0, bytes_accessed=0, transcendentals=0),
    )(place, parents, *[kv[s] for s in KV_ORDER], *packs, *rest)


def total_kernel(grad_own, *refs):
    parts, (total, _, side, sem) = refs[: RING - 1], refs[RING + 2 :]
    value = grad_own[...]
    for part in parts:
        value = value + part[...].astype(F32)
    total[...] = value.astype(BF16)
    store = pltpu.make_async_copy(
        total.at[pl.ds(4 * BLK, 4 * BLK), :], side.at[pl.ds(2 * ROWS, 4 * BLK), :], sem
    )
    store.start()
    store.wait()


def total_call(grad_own, received, inputs, side, after):
    hbm = pl.BlockSpec(memory_space=pl.ANY)
    return pl.pallas_call(
        total_kernel,
        out_shape=[shape(ROWS), shape(*inputs.shape), shape(*side.shape)],
        in_specs=[vmem()] * RING + [hbm] * 3,
        out_specs=[vmem(), hbm, hbm],
        scratch_shapes=[pltpu.SemaphoreType.DMA],
        input_output_aliases={RING: 1, RING + 1: 2},
        compiler_params=pltpu.CompilerParams(vmem_limit_bytes=16 * MIB),
        cost_estimate=pl.CostEstimate(flops=0, bytes_accessed=0, transcendentals=0),
    )(grad_own, *received, inputs, side, after)


def relay_kernel(near, side, total, *rest):
    out = rest[-1]
    out[0:ROWS, :] = side[ROWS : 2 * ROWS, :]
    out[ROWS : ROWS + 2 * BLK, :] = total[2 * BLK : 4 * BLK, :]
    out[ROWS + 2 * BLK : ROWS + 4 * BLK, :] = side[2 * ROWS + 2 * BLK :, :]
    out[ROWS + 4 * BLK :, :] = near[ROWS:, :]


def join_inputs_kernel(*refs):
    pieces, out = refs[:RING], refs[-1]
    for s, piece in zip((0,) + RING_ORDER, pieces):
        out[s * BLK : (s + 1) * BLK, :] = piece[...]


def projection_kernel(*refs):
    grads = dict(zip((0,) + RING_ORDER, refs[:RING]))
    inputs = refs[RING : RING + SIDE]
    out, grad_t, weight_t, keys, values = refs[RING + SIDE :]
    for s in range(RING):
        for k in range(SIDE):
            at = 2 * k * BLK
            grad_t[k, 0:BLK, s * BLK : (s + 1) * BLK] = grads[s][at : at + BLK, :].T
            grad_t[k, BLK:, s * BLK : (s + 1) * BLK] = grads[s][at + BLK : at + 2 * BLK, :].T
    total = jnp.dot(grad_t[0], inputs[0][...], preferred_element_type=F32)
    for k in range(1, SIDE):
        total = total + jnp.dot(grad_t[k], inputs[k][...], preferred_element_type=F32)
    weight_t[...] = total
    for n in range(keys.shape[0] // BLK):
        rows = slice(n * BLK, (n + 1) * BLK)
        keys[rows, :] = weight_t[0:BLK, rows].T
        values[rows, :] = weight_t[BLK:, rows].T
    count, both, _ = out.shape
    for j in range(count):
        rows = slice(j * (both // 2), (j + 1) * (both // 2))
        out[j] = jnp.concatenate([keys[rows, :], values[rows, :]], axis=0).astype(BF16)


def weight_kernel(parts, out):
    share = out.shape[0]
    for g in range(KEY_VALUE_HEADS):
        total = parts[g].astype(F32)
        for d in range(1, TREES):
            total = total + parts[d * SIDE + g].astype(F32)
        out[:, g * HEAD_SIZE : (g + 1) * HEAD_SIZE] = total[0:share]
        col = (KEY_VALUE_HEADS + g) * HEAD_SIZE
        out[:, col : col + HEAD_SIZE] = total[share:]


def join_kernel(place, near, side, crossed, total, queries, keys, values):
    own = place[1]
    kv_at = ROWS + 4 * BLK
    for h in range(GROUP):
        rows = slice(h * BLK, (h + 1) * BLK)
        last = slice(kv_at + h * BLK, kv_at + (h + 1) * BLK)
        for k, piece in enumerate((near[rows, :], crossed[last, :], side[rows, :], crossed[rows, :])):
            col = pl.multiple_of((own ^ k) * (GROUP * HEAD_SIZE) + h * HEAD_SIZE, HEAD_SIZE)
            queries[:, pl.ds(col, HEAD_SIZE)] = piece
    for k, (ref, at) in enumerate(((total, 0), (crossed, ROWS), (side, 2 * ROWS), (crossed, ROWS + 2 * BLK))):
        col = pl.multiple_of((own ^ k) * HEAD_SIZE, HEAD_SIZE)
        keys[:, pl.ds(col, HEAD_SIZE)] = ref[at : at + BLK, :]
        values[:, pl.ds(col, HEAD_SIZE)] = ref[at + BLK : at + 2 * BLK, :]


def shape(rows, cols=HEAD_SIZE, kind=BF16):
    return jax.ShapeDtypeStruct((rows, cols), kind)


def local(
    queries,
    key_tensor,
    value_tensor,
    attention_output,
    output_gradient,
    logsumexp_rows,
    layer_input,
    parents,
    trees,
):
    width = layer_input.shape[2]
    quarter = width // RING
    share = width // (trees * RING * SIDE)
    at = lax.axis_index("ctx")
    ring, own = at // SIDE, at % SIDE
    place = jnp.stack([ring, own]).astype(jnp.int32)

    def to_side(x, k):
        return lax.ppermute(x, "ctx", side_perm(k))

    def to_ring(x, s):
        return lax.ppermute(x, "ctx", ring_perm(s % RING))

    query_args = (queries[0], output_gradient[0], attention_output[0], logsumexp_rows[0])
    with jax.named_scope("near"):
        near_own = split_queries(place, *query_args, 0, key_tensor[0], value_tensor[0])
        packs_near = [near_own[0], to_side(near_own[1], 1)]
        kv_first = near_own[3]
        kv_far = [to_side(near_own[2 + k], k) for k in (2, 3)]

    with jax.named_scope("keys_values_ring"):
        kv_own, token = pl.pallas_call(
            stack_kernel,
            out_shape=[shape(ROWS), shape(8, 128, F32)],
            in_specs=[vmem()] * SIDE,
            out_specs=[vmem(), pl.BlockSpec(memory_space=pl.ANY)],
            compiler_params=pltpu.CompilerParams(vmem_limit_bytes=20 * MIB),
            cost_estimate=pl.CostEstimate(flops=0, bytes_accessed=0, transcendentals=0),
        )(kv_first, packs_near[1], *kv_far)
        kv = {s: to_ring(kv_own, s) for s in RING_ORDER}
        kv = [kv_own] + [kv[s] for s in (1, 2, 3)]

    with jax.named_scope("queries_far"):
        far_own = split_queries(place, *query_args, 2, near_own[2])
        packs_far = [to_side(far_own[k - 2], k) for k in (2, 3)]

    with jax.named_scope("inputs_ring"):
        shares = call(
            share_inputs_kernel,
            [shape(BLK, quarter)] * RING,
            1,
            1,
            n_any=4,
            scratch=[pltpu.VMEM((RING, BLK, quarter), BF16)],
        )(place, layer_input[0], kv[1], kv[3], kv[2], packs_near[1])
        from_ring = [shares[0]] + [to_ring(shares[s], s) for s in RING_ORDER]

    with jax.named_scope("attention_near"):
        dq_near, sums = attention_call(place, parents, kv, packs_near, 0)

    with jax.named_scope("inputs_side"):
        input_own = call(join_inputs_kernel, [shape(RING * BLK, quarter)], 0, RING, n_any=3)(
            *from_ring, *packs_far, dq_near
        )[0]
        input_y = to_side(input_own, 2)
        input_core = to_side(input_own, 1)

    with jax.named_scope("attention_far"):
        outs = attention_call(place, parents, kv, packs_far, 2, sums, input_own)
        side_out, grad_own, grad_parts = outs[0], outs[1], outs[2:]

    with jax.named_scope("kv_gradients"):
        received = [to_ring(grad_parts[s - 1], -s) for s in RING_ORDER]
        grad_total, input_y, side_out = total_call(grad_own, received, input_y, side_out, input_core)
        input_last = to_side(input_y, 1)
        grads = [grad_total] + [to_ring(grad_total, s) for s in RING_ORDER]

    with jax.named_scope("projection"):
        partial = call(
            projection_kernel,
            [jax.ShapeDtypeStruct((trees * SIDE, 2 * share, HEAD_SIZE), BF16)],
            0,
            RING + SIDE,
            scratch=[
                pltpu.VMEM((SIDE, 2 * BLK, RING * BLK), BF16),
                pltpu.VMEM((2 * BLK, quarter), F32),
                pltpu.VMEM((quarter, HEAD_SIZE), F32),
                pltpu.VMEM((quarter, HEAD_SIZE), F32),
            ],
        )(*grads, input_own, input_core, input_y, input_last)[0]

    with jax.named_scope("own_gradients"):
        side = to_side(side_out, 2)
        crossed = to_side(
            call(relay_kernel, [shape(2 * ROWS + 4 * BLK)], 0, 3, n_any=3)(dq_near, side, grad_total, *grads[:0:-1])[0], 1
        )
        grad_queries, grad_keys, grad_values = call(
            join_kernel,
            [shape(BLK, QUERY_HEADS * HEAD_SIZE)] + [shape(BLK, KEY_VALUE_HEADS * HEAD_SIZE)] * 2,
            1,
            4,
            moved=64 * MIB,
        )(place, dq_near, side, crossed, grad_total)

    with jax.named_scope("projection_sum"):
        groups = [
            [d * RING * SIDE + r * SIDE + g for d in range(trees) for g in range(SIDE)]
            for r in range(RING)
        ]
        swapped = lax.all_to_all(partial, ("dp", "ctx"), 0, 0, axis_index_groups=groups, tiled=True)
        grad_kv_weight = call(weight_kernel, [shape(share, 2 * KEY_VALUE_HEADS * HEAD_SIZE, F32)], 0, 1)(swapped)[0]

    return grad_queries[None], grad_keys[None], grad_values[None], grad_kv_weight


def solution(mesh):
    in_specs = (
        P("dp", "ctx", None),
        P("dp", "ctx", None),
        P("dp", "ctx", None),
        P("dp", "ctx", None),
        P("dp", "ctx", None),
        P("dp", None, "ctx"),
        P("dp", "ctx", None),
        P("dp", None),
    )
    out_specs = (
        P("dp", "ctx", None),
        P("dp", "ctx", None),
        P("dp", "ctx", None),
        P(("dp", "ctx"), None),
    )
    return jax.shard_map(
        functools.partial(local, trees=mesh.shape["dp"]),
        mesh=mesh,
        in_specs=in_specs,
        out_specs=out_specs,
        check_vma=False,
    )
```
